512 devices in a mesh: seq: 32 (over y, z_lo), tp: 16 (over z_hi, x, core).
Axes of the slice: x: 4, y: 8, z: 8 (z_hi: 2, z_lo: 4; z = z_hi * 4 + z_lo), core: 2. Of those that a mesh axis runs over, the one named last changes fastest.
Arguments:
- query_two: bfloat16 [4096, 4096], P('seq', 'tp'), may hold values from -128 to 128
- key_two: bfloat16 [4096, 4096], P('seq', 'tp'), may hold values from -6 to 6
- value_two: bfloat16 [4096, 4096], P('seq', 'tp'), may hold values from -6 to 6
- cotangent_two: bfloat16 [4096, 5120], P('seq', 'tp'), may hold values from -6 to 6
- kept_two: int32 [4096], P('seq'), may hold values from -1 to 16383, as said below
- query_three: bfloat16 [2048, 4096], P('seq', 'tp'), may hold values from -128 to 128
- key_three: bfloat16 [2048, 4096], P('seq', 'tp'), may hold values from -6 to 6
- value_three: bfloat16 [2048, 4096], P('seq', 'tp'), may hold values from -6 to 6
- cotangent_three: bfloat16 [2048, 5120], P('seq', 'tp'), may hold values from -6 to 6
- kept_three: int32 [2048], P('seq'), may hold values from -1 to 16383, as said below
- out_weight: bfloat16 [4096, 5120], P('tp'), may hold values from -0.09375 to 0.09375
Outputs:
- grad_query_two: bfloat16 [4096, 4096], P('seq', 'tp')
- grad_key_two: bfloat16 [4096, 4096], P('seq', 'tp')
- grad_value_two: bfloat16 [4096, 4096], P('seq', 'tp')
- grad_query_three: bfloat16 [2048, 4096], P('seq', 'tp')
- grad_key_three: bfloat16 [2048, 4096], P('seq', 'tp')
- grad_value_three: bfloat16 [2048, 4096], P('seq', 'tp')
The draws below stay inside these ranges and needn't reach their ends.
Inputs may be any that keep to these rules, and one draw needn't show every extreme that they name: `kept_two`: index k of seq holds slots k * 128 to (k+1) * 128 - 1: kept positions from k * 512 to (k+1) * 512 - 1 in increasing order, then -1 for empty slots; 64 or more live slots on each index, all 128 live on some index. `kept_three`: positions also kept at depth two, in blocks of 128 slots; block k takes its positions from those of seq indices 2 * k and 2 * k + 1, increasing, live slots first and -1 after; some block is full.
All inputs are finite; a program needn't handle non-finite values.
Results may differ from the reference program's by a relative error of at most 0.01.
Values may be sent and summed in bfloat16 or wider, within the bound.
A program may use at most 64 MiB of HBM per device.

```python
import math
import jax
import jax.numpy as jnp
from jax import lax

D = 5120
HEADS = 32
HEAD_DIM = 128
TOK_DEV = 512
SLOTS = 128
WIDTH = 4096
ROWS2 = 4096
ROWS3 = 2048


def query_key_rows(key, salt, row_count):
    key = jax.random.fold_in(key, salt)
    first_key, second_key = jax.random.split(key, 2)
    width = HEADS * HEAD_DIM
    queries = jnp.clip(jax.random.normal(first_key, (row_count, width), jnp.float32), -6.0, 6.0)
    keys_drawn = jnp.clip(jax.random.normal(second_key, (row_count, width), jnp.float32), -6.0, 6.0)
    return (queries, keys_drawn)


def kept_lists(key):
    key = jax.random.fold_in(key, 31)
    count_key, pick_key, order_key, third_count, third_pick, third_order = jax.random.split(key, 6)
    devices = ROWS2 // SLOTS
    pairs = devices // 2
    slot_ids = jnp.arange(SLOTS)[None, :]
    live_two = jax.random.randint(count_key, (devices,), SLOTS // 2, SLOTS + 1)
    full_device = jax.random.randint(pick_key, (), 0, devices)
    live_two = jnp.where(jnp.arange(devices) == full_device, SLOTS, live_two)
    shuffled = jax.vmap(lambda sub_key: jax.random.permutation(sub_key, TOK_DEV))(jax.random.split(order_key, devices))[:, :SLOTS]
    chosen = jnp.sort(jnp.where(slot_ids < live_two[:, None], shuffled, TOK_DEV), axis=1)
    offsets = (jnp.arange(devices) * TOK_DEV)[:, None]
    depth_two = jnp.where(chosen < TOK_DEV, chosen + offsets, -1)
    candidates = depth_two.reshape(pairs, 2 * SLOTS)
    candidate_live = candidates >= 0
    available = candidate_live.astype(jnp.int32).sum(axis=1)
    live_three = jax.random.randint(third_count, (pairs,), SLOTS // 8, SLOTS + 1)
    full_pair = jax.random.randint(third_pick, (), 0, pairs)
    live_three = jnp.where(jnp.arange(pairs) == full_pair, SLOTS, live_three)
    live_three = jnp.minimum(live_three, available)
    ranking = jax.vmap(lambda sub_key: jax.random.permutation(sub_key, 2 * SLOTS))(jax.random.split(third_order, pairs))
    ranking = jnp.where(candidate_live, ranking, ranking + 2 * SLOTS)
    ordering = jnp.argsort(ranking, axis=1)[:, :SLOTS]
    picked = jnp.take_along_axis(candidates, ordering, axis=1)
    beyond = devices * TOK_DEV
    picked = jnp.sort(jnp.where(slot_ids < live_three[:, None], picked, beyond), axis=1)
    depth_three = jnp.where(picked < beyond, picked, -1)
    return (depth_two.reshape(-1).astype(jnp.int32), depth_three.reshape(-1).astype(jnp.int32))


def draw_query_two(key, part):
    return query_key_rows(key, 11, ROWS2)[0].astype(jnp.bfloat16)


def draw_key_two(key, part):
    return query_key_rows(key, 11, ROWS2)[1].astype(jnp.bfloat16)


def draw_query_three(key, part):
    return query_key_rows(key, 12, ROWS3)[0].astype(jnp.bfloat16)


def draw_key_three(key, part):
    return query_key_rows(key, 12, ROWS3)[1].astype(jnp.bfloat16)


def draw_kept_two(key, part):
    return kept_lists(key)[0]


def draw_kept_three(key, part):
    return kept_lists(key)[1]


def block_scale(rng, shape, cuts, least, top_value):
    gain = 1.0
    for axis_at, shards_of in cuts:
        heights = jax.random.uniform(jax.random.fold_in(jax.random.fold_in(rng, 6), axis_at), (shards_of,), jnp.float32, least / len(cuts), top_value / len(cuts))
        gain = gain * jnp.repeat(jnp.exp(heights), shape[axis_at] // shards_of).reshape((-1,) + (1,) * (len(shape) - 1 - axis_at))
    return gain


def centred(rng, extent, scale, bound, cuts=(), held_as=jnp.bfloat16):
    array = scale * jax.random.normal(rng, extent, jnp.float32)
    if cuts:
        array = array * block_scale(rng, extent, cuts, -0.22, 0.18)
    return jnp.clip(array, -bound, bound).astype(held_as)


def setup_inputs(seed: int = 0) -> dict:
    splits = jax.random.split(jax.random.key(seed), 12)
    return {
        "query_two": draw_query_two(jax.random.fold_in(splits[11], 71), 0),
        "key_two": draw_key_two(jax.random.fold_in(splits[11], 71), 0),
        "value_two": centred(splits[2], (ROWS2, WIDTH), 1.0, 6.0, ((0, 32), (1, 16))),
        "cotangent_two": centred(splits[3], (ROWS2, D), 1.0, 6.0, ((0, 32), (1, 16))),
        "kept_two": draw_kept_two(jax.random.fold_in(splits[11], 71), 0),
        "query_three": draw_query_three(jax.random.fold_in(splits[11], 71), 0),
        "key_three": draw_key_three(jax.random.fold_in(splits[11], 71), 0),
        "value_three": centred(splits[7], (ROWS3, WIDTH), 1.0, 6.0, ((0, 32), (1, 16))),
        "cotangent_three": centred(splits[8], (ROWS3, D), 1.0, 6.0, ((0, 32), (1, 16))),
        "kept_three": draw_kept_three(jax.random.fold_in(splits[11], 71), 0),
        "out_weight": centred(splits[10], (WIDTH, D), WIDTH ** -0.5, 0.09375, ((0, 16),)),
    }


NEG = -1e+30

def depth_grads(query, keys, values, outer, kept):
    row_count = query.shape[0]
    head_count = query.shape[1] // HEAD_DIM
    scaling = 1.0 / math.sqrt(HEAD_DIM)
    live_rows = kept >= 0
    allowed = live_rows[:, None] & live_rows[None, :] & (kept[None, :] <= kept[:, None])

    def one_head(head_id):
        offset = (head_id * HEAD_DIM).astype(jnp.int32)
        query_head = lax.dynamic_slice_in_dim(query, offset, HEAD_DIM, 1)
        key_head = lax.dynamic_slice_in_dim(keys, offset, HEAD_DIM, 1)
        value_head = lax.dynamic_slice_in_dim(values, offset, HEAD_DIM, 1)
        outer_head = lax.dynamic_slice_in_dim(outer, offset, HEAD_DIM, 1)
        scores = jnp.dot(query_head, key_head.T, preferred_element_type=jnp.float32) * scaling
        scores = jnp.where(allowed, scores, NEG)
        maximum = scores.max(axis=1, keepdims=True)
        weights = jnp.where(allowed, jnp.exp(scores - maximum), 0.0)
        row_total = jnp.where(live_rows, weights.sum(axis=1), 1.0)
        log_sum = jnp.where(live_rows, maximum[:, 0] + jnp.log(row_total), 0.0)
        probability = jnp.where(allowed, jnp.exp(scores - log_sum[:, None]), 0.0)
        grad_probs = jnp.dot(outer_head, value_head.T, preferred_element_type=jnp.float32)
        delta_sum = (probability * grad_probs).sum(axis=1)
        grad_scores = probability * (grad_probs - delta_sum[:, None])
        probability_low = probability.astype(jnp.bfloat16)
        grad_low = grad_scores.astype(jnp.bfloat16)
        grad_query = jnp.dot(grad_low, key_head, preferred_element_type=jnp.float32) * scaling
        grad_key = jnp.dot(grad_low.T, query_head, preferred_element_type=jnp.float32) * scaling
        grad_value = jnp.dot(probability_low.T, outer_head, preferred_element_type=jnp.float32)
        return (grad_query, grad_key, grad_value)
    stacked = lax.map(one_head, jnp.arange(head_count, dtype=jnp.int32))
    return tuple((member.transpose(1, 0, 2).reshape(row_count, head_count * HEAD_DIM).astype(jnp.bfloat16) for member in stacked))

def reference(query_two, key_two, value_two, cotangent_two, kept_two, query_three, key_three, value_three, cotangent_three, kept_three, out_weight):
    outer_two = jnp.dot(cotangent_two, out_weight.T, preferred_element_type=jnp.float32).astype(jnp.bfloat16)
    outer_three = jnp.dot(cotangent_three, out_weight.T, preferred_element_type=jnp.float32).astype(jnp.bfloat16)
    grads_two = depth_grads(query_two, key_two, value_two, outer_two, kept_two)
    grads_three = depth_grads(query_three, key_three, value_three, outer_three, kept_three)
    return (grads_two[0], grads_two[1], grads_two[2], grads_three[0], grads_three[1], grads_three[2])
```

```python
import functools
import math

import jax
import jax.numpy as jnp
from jax import lax
from jax.experimental import pallas as pl
from jax.experimental.pallas import tpu as pltpu
from jax.sharding import PartitionSpec as P

MESH = pl.DeviceIdType.MESH
F32, BF16 = jnp.float32, jnp.bfloat16
HEAD = 128
R2, R3 = 128, 64
RT = R2 + R3
FEAT = 320
NEG = -1e30
SCALE = 1.0 / math.sqrt(HEAD)
SLOT = 2 * RT + 16
GRAD = 2 * RT


def dot_nt(a, b):
    return lax.dot_general(a, b, (((1,), (1,)), ((), ())), preferred_element_type=F32)


def dot_nn(a, b):
    return lax.dot_general(a, b, (((1,), (0,)), ((), ())), preferred_element_type=F32)


def dot_tn(a, b):
    return lax.dot_general(a, b, (((0,), (0,)), ((), ())), preferred_element_type=F32)


def device(y, z, zh, x, c):
    return (y * 4 + z, (zh * 4 + x) * 2 + c)


def body(
    kept2, kept3, q2, k2, v2, cot2, q3, k3, v3, cot3, weight,
    dq2, dk2, dv2, dq3, dk3, dv3,
    cot, wv, kv, qb2, qb3, ob2, ob3, bias, ost, acc2, acc3, st2, st3,
    stat, stat_out, stat_in, rb, sb, tmp, dqt2, dqt3, dqx_out, dqx_in, dq_out, dq_in, back_out, back_in,
    ssem, lsem, cot_z, cot_x, cot_s, kvin, qin, oin, ring, red, ring_s, red_s, xsem, backsem, dqsem,
):
    s, t = lax.axis_index("seq"), lax.axis_index("tp")
    y, z = lax.div(s, 4), lax.rem(s, 4)
    zh, x, c = lax.div(t, 8), lax.rem(lax.div(t, 2), 4), lax.rem(t, 2)
    zhalf, zpar = lax.div(z, 2), lax.rem(z, 2)

    sent = []

    def send(src, dst, sem, to, when=None):
        copy = pltpu.make_async_remote_copy(
            src_ref=src, dst_ref=dst, send_sem=ssem.at[len(sent)], recv_sem=sem,
            device_id=to, device_id_type=MESH,
        )
        if when is None:
            copy.start()
        else:
            pl.when(when)(copy.start)
        sent.append((copy, when))

    def keep(src, dst, sem, when=None):
        copy = pltpu.make_async_copy(src, dst, sem)
        if when is None:
            copy.start()
        else:
            pl.when(when)(copy.start)

    def arrive(ref, sem):
        pltpu.make_async_copy(ref, ref, sem).wait()

    sibling = device(y, z, zh, x, 1 - c)
    y_up, y_down = lax.rem(y + 1, 8), lax.rem(y + 7, 8)

    barrier = pltpu.get_barrier_semaphore()
    peers = [device(y_up, z, zh, x, c), device(y_down, z, zh, x, c), device(y, z, 1 - zh, x, c), sibling]
    for dx in (1, 2, 3):
        peers.append(device(y, z, zh, lax.rem(x + dx, 4), c))
        for cc in (0, 1):
            peers.append(device(y, lax.rem(z + dx, 4), zh, x, cc))
    for peer in peers:
        pl.semaphore_signal(barrier, inc=1, device_id=peer, device_id_type=MESH)
    keep(cot2, cot.at[zh, x, c, 0:R2], lsem.at[0])
    keep(cot3, cot.at[zh, x, c, R2:RT], lsem.at[1])
    keep(weight, wv, lsem.at[2])
    rows = lax.broadcasted_iota(jnp.int32, (16, HEAD), 0)
    live2 = jnp.where(kept2[...] >= 0, 0.0, NEG)
    live3 = jnp.where(kept3[...] >= 0, 0.0, NEG)
    bias_value = jnp.where(rows == 0, live2, jnp.where(rows == 1, live3, 0.0))
    bias[...] = bias_value.astype(BF16)
    stat[...] = jnp.where(lax.broadcasted_iota(jnp.int32, stat.shape, 0) == 0, NEG, 0.0)
    acc2[...] = jnp.zeros_like(acc2)
    acc3[...] = jnp.zeros_like(acc3)
    dqt2[...] = jnp.zeros_like(dqt2)
    dqt3[...] = jnp.zeros_like(dqt3)
    pl.semaphore_wait(barrier, len(peers))

    far = device(y, z, 1 - zh, x, c)
    mine = cot.at[zh, x, c]
    send(cot2, mine.at[0:R2], cot_z.at[0], far)
    send(cot3, mine.at[R2:RT], cot_z.at[1], far)

    for hh in (0, 1):
        cols = pl.ds(hh * HEAD, HEAD)
        here = (zhalf == c) & (zpar == hh)
        away = jnp.logical_not(here)
        to = device(y, 2 * c + hh, zh, x, zhalf)
        slot = kv.at[y, zpar]
        sem = kvin.at[zpar]
        parts = (
            (k2.at[:, cols], slot.at[0:R2]),
            (k3.at[:, cols], slot.at[R2:RT]),
            (v2.at[:, cols], slot.at[RT:RT + R2]),
            (v3.at[:, cols], slot.at[RT + R2:GRAD]),
            (bias, slot.at[GRAD:SLOT]),
        )
        for src, dst in parts:
            keep(src, dst, sem, here)
            send(src, dst, sem, to, away)

    for dx in (1, 3, 2):
        to = device(y, z, zh, lax.rem(x + dx, 4), c)
        send(cot2, mine.at[0:R2], cot_x.at[0, x], to)
        send(cot3, mine.at[R2:RT], cot_x.at[0, x], to)
    send(cot2, mine.at[0:R2], cot_s.at[zh, x], sibling)
    send(cot3, mine.at[R2:RT], cot_s.at[zh, x], sibling)

    at2 = pl.ds(pl.multiple_of(z * R2, R2), R2)
    at3 = pl.ds(pl.multiple_of(z * R3, R3), R3)

    def to_workers(hh, part2, part3, dst2, dst3, sems):
        for cc in (0, 1):
            here = (z == 2 * c + hh) & (c == cc)
            away = jnp.logical_not(here)
            to = device(y, 2 * c + hh, zh, x, cc)
            for depth, (src, dst) in enumerate(((part2, dst2.at[at2]), (part3, dst3.at[at3]))):
                keep(src, dst, sems.at[z, depth], here)
                send(src, dst, sems.at[z, depth], to, away)

    def from_sources(dst2, dst3, sems):
        for zz in range(4):
            arrive(dst2.at[zz * R2:(zz + 1) * R2], sems.at[zz, 0])
            arrive(dst3.at[zz * R3:(zz + 1) * R3], sems.at[zz, 1])

    for hh in (0, 1):
        cols = pl.ds(hh * HEAD, HEAD)
        to_workers(hh, q2.at[:, cols], q3.at[:, cols], qb2, qb3, qin)

    ring_to = (device(y_up, z, zh, x, c), device(y_down, z, zh, x, c))

    def origin(direction, step):
        return lax.rem(y + (8 - step if direction == 0 else step), 8)

    ring_sent = []

    def ring_send(direction, step, sub, at):
        slot = kv.at[at, sub]
        copy = pltpu.make_async_remote_copy(
            src_ref=slot, dst_ref=slot, send_sem=ring_s.at[direction, step, sub], recv_sem=ring.at[direction, step, sub],
            device_id=ring_to[direction], device_id_type=MESH,
        )
        copy.start()
        ring_sent.append(copy)

    def ring_step(step):
        for sub in (0, 1):
            for direction in (0, 1):
                if step == 4 and sub != direction:
                    continue
                at = origin(direction, step)
                arrive(kv.at[at, sub], ring.at[direction, step - 1, sub])
                if step < 3 or (step == 3 and sub == direction):
                    ring_send(direction, step, sub, at)

    row2 = pl.ds(0, 512)
    row3 = pl.ds(512, 256)

    def early_part(at, sub, rows_k, rows_v, queries, column, row, store, acc, base):
        scores = dot_nt(kv[at, sub, rows_k], queries[...]) * SCALE
        key_slot = lax.broadcasted_iota(jnp.int32, scores.shape, 0) + base
        query_slot = lax.broadcasted_iota(jnp.int32, scores.shape, 1)
        scores = jnp.where(key_slot <= query_slot, scores + column, NEG)
        store[at * 2 + sub] = scores
        before = stat[0:1, row]
        now = jnp.maximum(before, jnp.max(scores, axis=0, keepdims=True))
        weights = jnp.exp(scores - now)
        fade = jnp.exp(before - now)
        stat[0:1, row] = now
        stat[1:2, row] = stat[1:2, row] * fade + jnp.sum(weights, axis=0, keepdims=True)
        acc[...] = acc[...] * fade + dot_tn(kv[at, sub, rows_v], weights.astype(BF16))

    def early(at, sub):
        @pl.when(at <= y)
        def _():
            line = kv[at, sub, GRAD:SLOT].astype(F32)
            column = jnp.concatenate([line, jnp.zeros((HEAD - 16, HEAD), F32)], axis=0).T
            part = 2 * c + sub
            early_part(at, sub, pl.ds(0, R2), pl.ds(RT, R2), qb2, column[:, 0:1], row2, st2, acc2,
                       (at - y) * 512 + part * R2)
            early_part(at, sub, pl.ds(R2, R3), pl.ds(RT + R2, R3), qb3, column[0:R3, 1:2], row3, st3, acc3,
                       (at - y) * 256 + part * R3)

    def early_step(step):
        @pl.loop(0, 2 if step in (0, 4) else 4)
        def _(j):
            sub = lax.rem(j, 2)
            if step == 0:
                early(y, sub)
            elif step == 4:
                early(lax.rem(y + 4, 8), sub)
            else:
                forward = lax.div(j, 2)
                early(lax.rem(y + 8 + (2 * forward - 1) * step, 8), sub)

    arrive(kv.at[y, 0], kvin.at[0])
    arrive(kv.at[y, 1], kvin.at[1])
    for sub in (0, 1):
        for direction in (0, 1):
            ring_send(direction, 0, sub, y)

    for dx in (1, 3, 2):
        xx = lax.rem(x + dx, 4)
        arrive(cot.at[zh, xx, c], cot_x.at[0, xx])
        send(cot.at[zh, xx, c], cot.at[zh, xx, c], cot_s.at[zh, xx], sibling)
    from_sources(qb2, qb3, qin)
    early_step(0)

    other = cot.at[1 - zh, x, c]
    for piece, rows_p in enumerate((pl.ds(0, R2), pl.ds(R2, R3))):
        arrive(other.at[rows_p], cot_z.at[piece])
        for dx in (1, 3, 2):
            to = device(y, z, zh, lax.rem(x + dx, 4), c)
            send(other.at[rows_p], other.at[rows_p], cot_x.at[1, x], to)
    send(other, other, cot_s.at[1 - zh, x], sibling)

    ring_step(1)
    early_step(1)
    ring_step(2)
    early_step(2)
    for dx in (1, 3, 2):
        xx = lax.rem(x + dx, 4)
        theirs = cot.at[1 - zh, xx, c]
        arrive(theirs, cot_x.at[1, xx])
        send(theirs, theirs, cot_s.at[1 - zh, xx], sibling)
    ring_step(3)

    for zz in (0, 1):
        for xx in range(4):
            arrive(cot.at[zz, xx, 1 - c], cot_s.at[zz, xx])
    arrive(mine.at[0:R2], lsem.at[0])
    arrive(mine.at[R2:RT], lsem.at[1])
    arrive(wv, lsem.at[2])

    def project(p, total):
        zz, xx = lax.div(p, 4), lax.rem(p, 4)
        features = jnp.concatenate([cot[zz, xx, 0], cot[zz, xx, 1]], axis=1)
        return total + dot_nt(features, wv[:, pl.ds(pl.multiple_of(p * 2 * FEAT, HEAD), 2 * FEAT)])

    outer = lax.fori_loop(0, 8, project, jnp.zeros((RT, 2 * HEAD), F32))
    lines = jnp.concatenate([bias_value, jnp.zeros((HEAD - 16, HEAD), F32)], axis=0).T
    dead = jnp.concatenate([lines[:, 0:1], lines[0:R3, 1:2]], axis=0)
    outer = jnp.where(dead < 0.0, 0.0, outer).astype(BF16)
    for hh in (0, 1):
        ost[hh] = outer[:, hh * HEAD:(hh + 1) * HEAD]
        to_workers(hh, ost.at[hh, 0:R2], ost.at[hh, R2:RT], ob2, ob3, oin)

    early_step(3)
    ring_step(4)
    early_step(4)
    from_sources(ob2, ob3, oin)

    stat_out[...] = stat[...]
    stat_out[2:3, row2] = jnp.sum(ob2[...].astype(F32).T * acc2[...], axis=0, keepdims=True)
    stat_out[2:3, row3] = jnp.sum(ob3[...].astype(F32).T * acc3[...], axis=0, keepdims=True)
    send(stat_out, stat_in, xsem.at[0], sibling)
    arrive(stat_in, xsem.at[0])
    top = jnp.maximum(stat_out[0:1], stat_in[0:1])
    own_part, other_part = jnp.exp(stat_out[0:1] - top), jnp.exp(stat_in[0:1] - top)
    total = stat_out[1:2] * own_part + stat_in[1:2] * other_part
    stat[3:4] = top + jnp.log(total)
    stat[4:5] = (stat_out[2:3] * own_part + stat_in[2:3] * other_part) / total

    def late_part(at, sub, rows_k, rows_v, queries, outers, row, store, dqt):
        probability = jnp.exp(store[at * 2 + sub] - stat[3:4, row])
        grad_probs = dot_nt(kv[at, sub, rows_v], outers[...])
        grad_low = (probability * (grad_probs - stat[4:5, row])).astype(BF16)
        tmp[rows_k] = dot_nn(grad_low, queries[...]) * SCALE
        tmp[rows_v] = dot_nn(probability.astype(BF16), outers[...])
        half = grad_low.shape[1] // 2
        for h in (0, 1):
            dqt[h] += dot_tn(kv[at, sub, rows_k], grad_low[:, h * half:(h + 1) * half])

    def late(at, sub):
        @pl.when(at <= y)
        def _():
            late_part(at, sub, pl.ds(0, R2), pl.ds(RT, R2), qb2, ob2, row2, st2, dqt2)
            late_part(at, sub, pl.ds(R2, R3), pl.ds(RT + R2, R3), qb3, ob3, row3, st3, dqt3)

        @pl.when(at > y)
        def _():
            tmp[...] = jnp.zeros_like(tmp)

    def red_copy(direction, step, sub):
        return pltpu.make_async_remote_copy(
            src_ref=sb.at[direction, step, sub], dst_ref=rb.at[direction, step, sub],
            send_sem=red_s.at[direction, step, sub], recv_sem=red.at[direction, step, sub],
            device_id=ring_to[direction], device_id_type=MESH,
        )

    for step in range(4):
        for sub in (0, 1):
            for direction in (0, 1):
                if step == 0 and sub != direction:
                    continue
                ahead = 4 - step
                at = lax.rem(y + (ahead if direction == 0 else 8 - ahead), 8)
                late(at, sub)
                value = tmp[...]
                if step > 1 or (step == 1 and sub == direction):
                    arrive(rb.at[direction, step - 1, sub], red.at[direction, step - 1, sub])
                    value = value + rb[direction, step - 1, sub].astype(F32)
                sb[direction, step, sub] = value.astype(BF16)
                red_copy(direction, step, sub).start()

    own_rows = []
    for sub in (0, 1):
        late(y, sub)
        own_rows.append(tmp[...])
        back_out[sub] = tmp[...].astype(BF16)

    dqx_out[:, 0:256] = dqt2[1 - c].astype(BF16)
    dqx_out[:, 256:384] = dqt3[1 - c].astype(BF16)
    send(dqx_out, dqx_in, xsem.at[1], sibling)
    arrive(dqx_in, xsem.at[1])
    query_two = (dqt2[c] + dqx_in[:, 0:256].astype(F32)) * SCALE
    query_three = (dqt3[c] + dqx_in[:, 256:384].astype(F32)) * SCALE
    rows_two, rows_three = query_two.T.astype(BF16), query_three.T.astype(BF16)

    def to_source(sub, src, dst, sems):
        here = (z == 2 * c + sub)
        to = device(y, 2 * c + sub, zh, x, zhalf)
        away = jnp.logical_not(here & (zhalf == c))
        keep(src, dst.at[zpar], sems.at[zpar], jnp.logical_not(away))
        send(src, dst.at[zpar], sems.at[zpar], to, away)

    for sub in (0, 1):
        dq_out[sub, 0:R2] = rows_two[sub * R2:(sub + 1) * R2]
        dq_out[sub, R2:RT] = rows_three[sub * R3:(sub + 1) * R3]
        to_source(sub, dq_out.at[sub], dq_in, dqsem)

    for sub in (0, 1):
        value = own_rows[sub]
        for direction in (0, 1):
            arrive(rb.at[direction, 3, sub], red.at[direction, 3, sub])
            value = value + rb[direction, 3, sub].astype(F32)
        back_out[sub] = value.astype(BF16)
        to_source(sub, back_out.at[sub], back_in, backsem)

    for hh in (0, 1):
        cols = pl.ds(hh * HEAD, HEAD)
        arrive(dq_in.at[hh], dqsem.at[hh])
        dq2[:, cols] = dq_in[hh, 0:R2]
        dq3[:, cols] = dq_in[hh, R2:RT]
    for hh in (0, 1):
        cols = pl.ds(hh * HEAD, HEAD)
        arrive(back_in.at[hh], backsem.at[hh])
        dk2[:, cols] = back_in[hh, 0:R2]
        dk3[:, cols] = back_in[hh, R2:RT]
        dv2[:, cols] = back_in[hh, RT:RT + R2]
        dv3[:, cols] = back_in[hh, RT + R2:GRAD]

    for copy, when in sent:
        if when is None:
            copy.wait_send()
        else:
            pl.when(when)(copy.wait_send)
    for copy in ring_sent:
        copy.wait_send()
    for step in range(4):
        for sub in (0, 1):
            for direction in (0, 1):
                if step > 0 or sub == direction:
                    red_copy(direction, step, sub).wait_send()


def on_device(q2, k2, v2, cot2, kept2, q3, k3, v3, cot3, kept3, weight):
    any_spec = pl.BlockSpec(memory_space=pl.ANY)
    vmem = pl.BlockSpec(memory_space=pltpu.VMEM)
    dma = pltpu.SemaphoreType.DMA
    line2 = kept2.reshape(1, R2)
    line3 = jnp.concatenate([kept3, jnp.zeros((HEAD - R3,), kept3.dtype)]).reshape(1, HEAD)
    wide = jax.ShapeDtypeStruct((R2, 2 * HEAD), BF16)
    narrow = jax.ShapeDtypeStruct((R3, 2 * HEAD), BF16)
    return pl.pallas_call(
        body,
        out_shape=(wide, wide, wide, narrow, narrow, narrow),
        in_specs=[vmem, vmem] + [any_spec] * 9,
        out_specs=(vmem,) * 6,
        scratch_shapes=[
            pltpu.VMEM((2, 4, 2, RT, FEAT), BF16),
            pltpu.VMEM((2 * HEAD, 16 * FEAT), BF16),
            pltpu.VMEM((8, 2, SLOT, HEAD), BF16),
            pltpu.VMEM((512, HEAD), BF16),
            pltpu.VMEM((256, HEAD), BF16),
            pltpu.VMEM((512, HEAD), BF16),
            pltpu.VMEM((256, HEAD), BF16),
            pltpu.VMEM((16, HEAD), BF16),
            pltpu.VMEM((2, RT, HEAD), BF16),
            pltpu.VMEM((HEAD, 512), F32),
            pltpu.VMEM((HEAD, 256), F32),
            pltpu.VMEM((16, R2, 512), F32),
            pltpu.VMEM((16, R3, 256), F32),
            pltpu.VMEM((8, 768), F32),
            pltpu.VMEM((8, 768), F32),
            pltpu.VMEM((8, 768), F32),
            pltpu.VMEM((2, 4, 2, GRAD, HEAD), BF16),
            pltpu.VMEM((2, 4, 2, GRAD, HEAD), BF16),
            pltpu.VMEM((GRAD, HEAD), F32),
            pltpu.VMEM((2, HEAD, 256), F32),
            pltpu.VMEM((2, HEAD, 128), F32),
            pltpu.VMEM((HEAD, 384), BF16),
            pltpu.VMEM((HEAD, 384), BF16),
            pltpu.VMEM((2, RT, HEAD), BF16),
            pltpu.VMEM((2, RT, HEAD), BF16),
            pltpu.VMEM((2, GRAD, HEAD), BF16),
            pltpu.VMEM((2, GRAD, HEAD), BF16),
            dma((64,)),
            dma((3,)),
            dma((2,)),
            dma((2, 4)),
            dma((2, 4)),
            dma((2,)),
            dma((4, 2)),
            dma((4, 2)),
            dma((2, 4, 2)),
            dma((2, 4, 2)),
            dma((2, 4, 2)),
            dma((2, 4, 2)),
            dma((2,)),
            dma((2,)),
            dma((2,)),
        ],
        compiler_params=pltpu.CompilerParams(
            collective_id=0, has_side_effects=True, vmem_limit_bytes=48 * 1024 * 1024
        ),
        name="attention_backward",
    )(line2, line3, q2, k2, v2, cot2, q3, k3, v3, cot3, weight)


def solution(mesh):
    shard = P("seq", "tp")
    in_specs = (shard, shard, shard, shard, P("seq"), shard, shard, shard, shard, P("seq"), P("tp", None))
    return jax.shard_map(on_device, mesh=mesh, in_specs=in_specs, out_specs=(shard,) * 6, check_vma=False)
```

```python
import functools
import math

import jax
import jax.numpy as jnp
from jax import lax
from jax.experimental import pallas as pl
from jax.experimental.pallas import tpu as pltpu
from jax.sharding import PartitionSpec as P

MESH = pl.DeviceIdType.MESH
F32, BF16 = jnp.float32, jnp.bfloat16
HEAD = 128
R2, R3 = 128, 64
RT = R2 + R3
FEAT = 320
NEG = -1e30
SCALE = 1.0 / math.sqrt(HEAD)
SCALE_TWO = SCALE * math.log2(math.e)
SLOT = 2 * RT + 16
GRAD = 2 * RT


def dot_nt(a, b):
    return lax.dot_general(a, b, (((1,), (1,)), ((), ())), preferred_element_type=F32)


def dot_nn(a, b):
    return lax.dot_general(a, b, (((1,), (0,)), ((), ())), preferred_element_type=F32)


def dot_tn(a, b):
    return lax.dot_general(a, b, (((0,), (0,)), ((), ())), preferred_element_type=F32)


def device(y, z, zh, x, c):
    return (y * 4 + z, (zh * 4 + x) * 2 + c)


def body(
    kept2, kept3, q2, k2, v2, cot2, q3, k3, v3, cot3, weight,
    dq_got, back_got,
    ct2, ct3, line2, line3, wv, kv, qb2, qb3, qt2, qt3, ob2, ob3, bias, outer2, outer3, ost2, ost3, acc2, acc3, st2, st3,
    stat, stat_out, stat_in, rb, sb, tmp, dqt2, dqt3, dqx_out, dqx_in, dq_out, dq_in, back_out, back_in,
    ssem, lsem, cot_z, cot_x, cot_s, kvin, qin, oin, ring, red, ring_s, red_s, xsem, backsem, dqsem,
):
    s, t = lax.axis_index("seq"), lax.axis_index("tp")
    y, z = lax.div(s, 4), lax.rem(s, 4)
    zh, x, c = lax.div(t, 8), lax.rem(lax.div(t, 2), 4), lax.rem(t, 2)
    zhalf, zpar = lax.div(z, 2), lax.rem(z, 2)

    sent = []

    def send(src, dst, sem, to, when=None):
        copy = pltpu.make_async_remote_copy(
            src_ref=src, dst_ref=dst, send_sem=ssem.at[len(sent)], recv_sem=sem,
            device_id=to, device_id_type=MESH,
        )
        if when is None:
            copy.start()
        else:
            pl.when(when)(copy.start)
        sent.append((copy, when))

    def keep(src, dst, sem, when=None):
        copy = pltpu.make_async_copy(src, dst, sem)
        if when is None:
            copy.start()
        else:
            pl.when(when)(copy.start)

    def arrive(ref, sem):
        pltpu.make_async_copy(ref, ref, sem).wait()

    def ct2_at(zz, xx, cc):
        return ct2.at[zz, xx, pl.ds(pl.multiple_of(cc * FEAT, 64), FEAT)]

    sibling = device(y, z, zh, x, 1 - c)
    y_up, y_down = lax.rem(y + 1, 8), lax.rem(y + 7, 8)

    barrier = pltpu.get_barrier_semaphore()
    peers = [device(y_up, z, zh, x, c), device(y_down, z, zh, x, c), device(y, z, 1 - zh, x, c), sibling]
    for dx in (1, 2, 3):
        peers.append(device(y, z, zh, lax.rem(x + dx, 4), c))
        for cc in (0, 1):
            peers.append(device(y, lax.rem(z + dx, 4), zh, x, cc))
    for peer in peers:
        pl.semaphore_signal(barrier, inc=1, device_id=peer, device_id_type=MESH)
    keep(kept2, line2, lsem.at[3])
    keep(kept3, line3, lsem.at[4])
    keep(cot2, ct2_at(zh, x, c), lsem.at[0])
    keep(cot3, ct3.at[zh, x, c], lsem.at[1])
    keep(weight, wv, lsem.at[2])
    pl.semaphore_wait(barrier, len(peers))

    def clear():
        stat[...] = jnp.where(lax.broadcasted_iota(jnp.int32, stat.shape, 0) == 0, NEG, 0.0)
        for ref in (acc2, acc3, dqt2, dqt3, outer2, outer3):
            ref[...] = jnp.zeros_like(ref)

    far = device(y, z, 1 - zh, x, c)
    mine2, mine3 = ct2_at(zh, x, c), ct3.at[zh, x, c]
    def cot_far():
        send(cot2, mine2, cot_z.at[0], far)
        send(cot3, mine3, cot_z.at[1], far)

    def make_bias():
        arrive(line2, lsem.at[3])
        arrive(line3, lsem.at[4])
        rows = lax.broadcasted_iota(jnp.int32, (16, HEAD), 0)
        live2 = jnp.where(line2[...] >= 0, 0.0, NEG)
        live3 = jnp.where(line3[...] >= 0, 0.0, NEG)
        live3 = jnp.concatenate([live3, live3], axis=1)
        bias[...] = jnp.where(rows == 0, live2, jnp.where(rows == 1, live3, 0.0)).astype(BF16)

    def keys_send():
        slot = kv.at[y, zpar]
        sem = kvin.at[zpar]

        def each(parts):
            for hh in (0, 1):
                here = (zhalf == c) & (zpar == hh)
                away = jnp.logical_not(here)
                to = device(y, 2 * c + hh, zh, x, zhalf)
                for src, dst in parts(pl.ds(hh * HEAD, HEAD)):
                    keep(src, dst, sem, here)
                    send(src, dst, sem, to, away)

        each(lambda cols: (
            (k2.at[:, cols], slot.at[0:R2]),
            (k3.at[:, cols], slot.at[R2:RT]),
            (v2.at[:, cols], slot.at[RT:RT + R2]),
            (v3.at[:, cols], slot.at[RT + R2:GRAD]),
        ))
        make_bias()
        each(lambda cols: ((bias, slot.at[GRAD:SLOT]),))

    def cot_near():
        for dx in (1, 3, 2):
            to = device(y, z, zh, lax.rem(x + dx, 4), c)
            send(cot2, mine2, cot_x.at[0, 0, x], to)
            send(cot3, mine3, cot_x.at[1, 0, x], to)
        send(cot2, mine2, cot_s.at[0, zh, x], sibling)
        send(cot3, mine3, cot_s.at[1, zh, x], sibling)

    def cot_arrive(zz, xx, kind):
        for depth, ref in enumerate((ct2_at(zz, xx, c), ct3.at[zz, xx, c])):
            arrive(ref, cot_x.at[depth, kind, xx])
            send(ref, ref, cot_s.at[depth, zz, xx], sibling)

    def rows2(zz):
        return pl.ds(pl.multiple_of(zz * R2, R2), R2)

    def rows3(zz):
        return pl.ds(pl.multiple_of(zz * R3, R3), R3)

    def to_workers(hh, parts, places, sems):
        here = (zhalf == c) & (zpar == hh)
        away = jnp.logical_not(here)
        to = device(y, 2 * c + hh, zh, x, zhalf)
        for depth, (src, dst) in enumerate(zip(parts, places(z))):
            keep(src, dst, sems.at[z, depth], here)
            send(src, dst, sems.at[z, depth], to, away)

    def hand_on(places, sems):
        for k in (0, 1):
            for depth, ref in enumerate(places(2 * c + k)):
                sem = sems.at[2 * c + k, depth]
                arrive(ref, sem)
                send(ref, ref, sem, sibling)

    def handed(places, sems):
        for k in (0, 1):
            for depth, ref in enumerate(places(2 * (1 - c) + k)):
                arrive(ref, sems.at[2 * (1 - c) + k, depth])

    def query_places(zz):
        return qb2.at[rows2(zz)], qb3.at[rows3(zz)]

    def outer_places(zz):
        return ob2.at[:, rows2(zz)], ob3.at[rows3(zz)]

    def queries_send():
        for hh in (0, 1):
            cols = pl.ds(hh * HEAD, HEAD)
            to_workers(hh, (q2.at[:, cols], q3.at[:, cols]), query_places, qin)

    ring_to = (device(y_up, z, zh, x, c), device(y_down, z, zh, x, c))

    def origin(direction, step):
        return lax.rem(y + (8 - step if direction == 0 else step), 8)

    ring_sent = []

    def ring_send(direction, step, sub, at):
        slot = kv.at[at, sub]
        copy = pltpu.make_async_remote_copy(
            src_ref=slot, dst_ref=slot, send_sem=ring_s.at[direction, step, sub], recv_sem=ring.at[direction, step, sub],
            device_id=ring_to[direction], device_id_type=MESH,
        )
        copy.start()
        ring_sent.append(copy)

    def ring_step(step):
        for sub in (0, 1):
            for direction in (0, 1):
                if step == 4 and sub != direction:
                    continue
                at = origin(direction, step)
                arrive(kv.at[at, sub], ring.at[direction, step - 1, sub])
                if step < 3 or (step == 3 and sub == direction):
                    ring_send(direction, step, sub, at)

    row2 = pl.ds(0, 512)
    row3 = pl.ds(512, 256)

    def both(at, rows):
        return jnp.concatenate([kv[at, 0, rows], kv[at, 1, rows]], axis=0)

    def early_part(at, rows_k, rows_v, queries, column, row, store, acc, first):
        scores = dot_nn(both(at, rows_k), queries[...]) * SCALE_TWO + column
        if first is not None:
            key_slot = lax.broadcasted_iota(jnp.int32, scores.shape, 0) + first
            query_slot = lax.broadcasted_iota(jnp.int32, scores.shape, 1)
            scores = jnp.where(key_slot <= query_slot, scores, NEG)
        store[at] = scores
        before = stat[0:1, row]
        now = jnp.maximum(before, jnp.max(scores, axis=0, keepdims=True))
        weights = jnp.exp2(scores - now)
        fade = jnp.exp2(before - now)
        stat[0:1, row] = now
        stat[1:2, row] = stat[1:2, row] * fade + jnp.sum(weights, axis=0, keepdims=True)
        acc[...] = acc[...] * fade + dot_tn(both(at, rows_v), weights.astype(BF16))

    def early_now(at, own):
        lines = [kv[at, sub, GRAD:SLOT].astype(F32) for sub in (0, 1)]
        turned = jnp.concatenate(lines + [jnp.zeros((HEAD - 32, HEAD), F32)], axis=0).T
        column2 = jnp.concatenate([turned[:, 0:1], turned[:, 16:17]], axis=0)
        column3 = jnp.concatenate([turned[0:R3, 1:2], turned[0:R3, 17:18]], axis=0)
        early_part(at, pl.ds(0, R2), pl.ds(RT, R2), qt2, column2, row2, st2, acc2, 2 * R2 * c if own else None)
        early_part(at, pl.ds(R2, R3), pl.ds(RT + R2, R3), qt3, column3, row3, st3, acc3, 2 * R3 * c if own else None)

    def early_step(step):
        if step == 0:
            early_now(y, True)
            return

        @pl.loop(0, 1 if step == 4 else 2)
        def _(forward):
            at = lax.rem(y + 8 + (2 * forward - 1) * step, 8)

            @pl.when(at < y)
            def _():
                early_now(at, False)

    def own_keys():
        arrive(kv.at[y, 0], kvin.at[0])
        arrive(kv.at[y, 1], kvin.at[1])
        for sub in (0, 1):
            for direction in (0, 1):
                ring_send(direction, 0, sub, y)

    def near_shards():
        for dx in (1, 3, 2):
            cot_arrive(zh, lax.rem(x + dx, 4), 0)

    def queries_over():
        hand_on(query_places, qin)

    def queries_here():
        handed(query_places, qin)
        qt2[...] = qb2[...].T
        qt3[...] = qb3[...].T

    def far_shard(depth):
        other = (ct2_at(1 - zh, x, c), ct3.at[1 - zh, x, c])[depth]
        arrive(other, cot_z.at[depth])
        for dx in (1, 3, 2):
            to = device(y, z, zh, lax.rem(x + dx, 4), c)
            send(other, other, cot_x.at[depth, 1, x], to)
        send(other, other, cot_s.at[depth, 1 - zh, x], sibling)

    def far_near_shards():
        for dx in (1, 3, 2):
            cot_arrive(1 - zh, lax.rem(x + dx, 4), 1)

    def project(zz):
        totals = [outer2[...], outer3[...]]
        for xx in range(4):
            part = wv[:, pl.ds(pl.multiple_of((zz * 4 + xx) * 2 * FEAT, HEAD), 2 * FEAT)]
            features = jnp.concatenate([ct3[zz, xx, 0], ct3[zz, xx, 1]], axis=1)
            totals[0] += dot_nn(part, ct2[zz, xx])
            totals[1] += dot_nt(part, features)
        outer2[...], outer3[...] = totals

    def sibling_shards(zz):
        for xx in range(4):
            arrive(ct2_at(zz, xx, 1 - c), cot_s.at[0, zz, xx])
            arrive(ct3.at[zz, xx, 1 - c], cot_s.at[1, zz, xx])

    def near_project():
        arrive(mine2, lsem.at[0])
        arrive(mine3, lsem.at[1])
        arrive(wv, lsem.at[2])
        sibling_shards(zh)
        project(zh)

    def far_project():
        sibling_shards(1 - zh)
        project(1 - zh)

    def outer_send():
        lines = bias[...].astype(F32)
        dead = jnp.concatenate([lines, jnp.zeros((HEAD - 16, HEAD), F32)], axis=0).T[0:R3, 1:2]
        part2 = jnp.where(lines[0:1] < 0.0, 0.0, outer2[...]).astype(BF16)
        part3 = jnp.where(dead < 0.0, 0.0, outer3[...].T).astype(BF16)
        for hh in (0, 1):
            ost2[hh] = part2[hh * HEAD:(hh + 1) * HEAD]
            ost3[hh] = part3[:, hh * HEAD:(hh + 1) * HEAD]
            to_workers(hh, (ost2.at[hh], ost3.at[hh]), outer_places, oin)

    def outer_here():
        hand_on(outer_places, oin)
        handed(outer_places, oin)

    keys_send()
    cot_far()
    cot_near()
    clear()
    own_keys()
    near_shards()
    queries_send()
    ring_step(1)
    far_shard(0)
    far_shard(1)
    queries_over()
    queries_here()
    early_step(0)
    ring_step(2)
    near_project()
    early_step(1)
    far_near_shards()
    ring_step(3)
    far_project()
    outer_send()
    early_step(2)
    ring_step(4)
    early_step(3)
    early_step(4)
    outer_here()

    stat_out[...] = stat[...]
    stat_out[2:3, row2] = jnp.sum(ob2[...].astype(F32) * acc2[...], axis=0, keepdims=True)
    stat_out[2:3, row3] = jnp.sum(ob3[...].astype(F32).T * acc3[...], axis=0, keepdims=True)
    send(stat_out, stat_in, xsem.at[0], sibling)
    arrive(stat_in, xsem.at[0])
    top = jnp.maximum(stat_out[0:1], stat_in[0:1])
    own_part, other_part = jnp.exp2(stat_out[0:1] - top), jnp.exp2(stat_in[0:1] - top)
    total = stat_out[1:2] * own_part + stat_in[1:2] * other_part
    stat[3:4] = top + jnp.log2(total)
    stat[4:5] = (stat_out[2:3] * own_part + stat_in[2:3] * other_part) / total

    def late_part(at, rows_k, rows_v, queries, outers, row, store, dqt, by_rows, by_columns):
        probability = jnp.exp2(store[at] - stat[3:4, row])
        grad_probs = by_rows(both(at, rows_v), outers[...])
        grad_low = (probability * (grad_probs - stat[4:5, row])).astype(BF16)
        keys = dot_nn(grad_low, queries[...]) * SCALE
        values = by_columns(probability.astype(BF16), outers[...])
        count = keys.shape[0] // 2
        for sub in (0, 1):
            tmp[sub, rows_k] = keys[sub * count:(sub + 1) * count]
            tmp[sub, rows_v] = values[sub * count:(sub + 1) * count]
        half = grad_low.shape[1] // 2
        for h in (0, 1):
            dqt[h] += dot_tn(both(at, rows_k), grad_low[:, h * half:(h + 1) * half])

    def late_now(at):
        late_part(at, pl.ds(0, R2), pl.ds(RT, R2), qb2, ob2, row2, st2, dqt2, dot_nn, dot_nt)
        late_part(at, pl.ds(R2, R3), pl.ds(RT + R2, R3), qb3, ob3, row3, st3, dqt3, dot_nt, dot_nn)

    def late(at):
        @pl.when(at < y)
        def _():
            late_now(at)

        @pl.when(at > y)
        def _():
            tmp[...] = jnp.zeros_like(tmp)

    def red_copy(direction, step, sub):
        return pltpu.make_async_remote_copy(
            src_ref=sb.at[direction, step, sub], dst_ref=rb.at[direction, step, sub],
            send_sem=red_s.at[direction, step, sub], recv_sem=red.at[direction, step, sub],
            device_id=device(lax.rem(y + 1 + 6 * direction, 8), z, zh, x, c), device_id_type=MESH,
        )

    late(lax.rem(y + 4, 8))
    for sub in (0, 1):
        sb[sub, 0, sub] = tmp[sub].astype(BF16)
        red_copy(sub, 0, sub).start()
    for step in (1, 2, 3):

        @pl.loop(0, 2)
        def _(direction):
            late(lax.rem(y + (4 - step) + direction * 2 * (4 + step), 8))
            for sub in (0, 1):

                def add():
                    arrive(rb.at[direction, step - 1, sub], red.at[direction, step - 1, sub])
                    tmp[sub] += rb[direction, step - 1, sub].astype(F32)

                if step == 1:
                    pl.when(direction == sub)(add)
                else:
                    add()
                sb[direction, step, sub] = tmp[sub].astype(BF16)
                red_copy(direction, step, sub).start()

    late_now(y)

    dqx_out[:, 0:256] = dqt2[1 - c].astype(BF16)
    dqx_out[:, 256:384] = dqt3[1 - c].astype(BF16)
    send(dqx_out, dqx_in, xsem.at[1], sibling)
    arrive(dqx_in, xsem.at[1])
    query_two = (dqt2[c] + dqx_in[:, 0:256].astype(F32)) * SCALE
    query_three = (dqt3[c] + dqx_in[:, 256:384].astype(F32)) * SCALE
    rows_two, rows_three = query_two.T.astype(BF16), query_three.T.astype(BF16)

    def to_source(sub, src, dst, sems):
        here = (z == 2 * c + sub)
        to = device(y, 2 * c + sub, zh, x, zhalf)
        away = jnp.logical_not(here & (zhalf == c))
        keep(src, dst.at[zpar], sems.at[zpar], jnp.logical_not(away))
        send(src, dst.at[zpar], sems.at[zpar], to, away)

    for sub in (0, 1):
        dq_out[sub, 0:R2] = rows_two[sub * R2:(sub + 1) * R2]
        dq_out[sub, R2:RT] = rows_three[sub * R3:(sub + 1) * R3]
        to_source(sub, dq_out.at[sub], dq_in, dqsem)

    for sub in (0, 1):
        value = tmp[sub]
        for direction in (0, 1):
            arrive(rb.at[direction, 3, sub], red.at[direction, 3, sub])
            value = value + rb[direction, 3, sub].astype(F32)
        back_out[sub] = value.astype(BF16)
        to_source(sub, back_out.at[sub], back_in, backsem)

    for hh in (0, 1):
        arrive(dq_in.at[hh], dqsem.at[hh])
    dq_got[...] = dq_in[...]
    for hh in (0, 1):
        arrive(back_in.at[hh], backsem.at[hh])
    back_got[...] = back_in[...]

    for copy, when in sent:
        if when is None:
            copy.wait_send()
        else:
            pl.when(when)(copy.wait_send)
    for copy in ring_sent:
        copy.wait_send()
    for step in range(4):
        for sub in (0, 1):
            for direction in (0, 1):
                if step > 0 or sub == direction:
                    red_copy(direction, step, sub).wait_send()


def lay_out(dq_got, back_got, dq2, dk2, dv2, dq3, dk3, dv3, sem):
    copies = []
    for hh in (0, 1):
        cols = pl.ds(hh * HEAD, HEAD)
        parts = (
            (back_got.at[hh, 0:R2], dk2),
            (back_got.at[hh, RT:RT + R2], dv2),
            (dq_got.at[hh, 0:R2], dq2),
            (back_got.at[hh, R2:RT], dk3),
            (back_got.at[hh, RT + R2:GRAD], dv3),
            (dq_got.at[hh, R2:RT], dq3),
        )
        for src, dst in parts:
            copies.append(pltpu.make_async_copy(src, dst.at[:, cols], sem.at[len(copies)]))
    for copy in copies:
        copy.start()
    for copy in copies:
        copy.wait()


def on_device(q2, k2, v2, cot2, kept2, q3, k3, v3, cot3, kept3, weight):
    hbm = pl.BlockSpec(memory_space=pltpu.HBM)
    vmem = pl.BlockSpec(memory_space=pltpu.VMEM)
    dma = pltpu.SemaphoreType.DMA
    line2 = kept2.reshape(1, R2)
    line3 = kept3.reshape(1, R3)
    got = pl.pallas_call(
        body,
        out_shape=(
            jax.ShapeDtypeStruct((2, RT, HEAD), BF16),
            jax.ShapeDtypeStruct((2, GRAD, HEAD), BF16),
        ),
        in_specs=[hbm] * 11,
        out_specs=(vmem,) * 2,
        scratch_shapes=[
            pltpu.VMEM((2, 4, 2 * FEAT, R2), BF16),
            pltpu.VMEM((2, 4, 2, R3, FEAT), BF16),
            pltpu.VMEM((1, R2), jnp.int32),
            pltpu.VMEM((1, R3), jnp.int32),
            pltpu.VMEM((2 * HEAD, 16 * FEAT), BF16),
            pltpu.VMEM((8, 2, SLOT, HEAD), BF16),
            pltpu.VMEM((512, HEAD), BF16),
            pltpu.VMEM((256, HEAD), BF16),
            pltpu.VMEM((HEAD, 512), BF16),
            pltpu.VMEM((HEAD, 256), BF16),
            pltpu.VMEM((HEAD, 512), BF16),
            pltpu.VMEM((256, HEAD), BF16),
            pltpu.VMEM((16, HEAD), BF16),
            pltpu.VMEM((2 * HEAD, R2), F32),
            pltpu.VMEM((2 * HEAD, R3), F32),
            pltpu.VMEM((2, HEAD, R2), BF16),
            pltpu.VMEM((2, R3, HEAD), BF16),
            pltpu.VMEM((HEAD, 512), F32),
            pltpu.VMEM((HEAD, 256), F32),
            pltpu.VMEM((8, 2 * R2, 512), F32),
            pltpu.VMEM((8, 2 * R3, 256), F32),
            pltpu.VMEM((8, 768), F32),
            pltpu.VMEM((8, 768), F32),
            pltpu.VMEM((8, 768), F32),
            pltpu.VMEM((2, 4, 2, GRAD, HEAD), BF16),
            pltpu.VMEM((2, 4, 2, GRAD, HEAD), BF16),
            pltpu.VMEM((2, GRAD, HEAD), F32),
            pltpu.VMEM((2, HEAD, 256), F32),
            pltpu.VMEM((2, HEAD, 128), F32),
            pltpu.VMEM((HEAD, 384), BF16),
            pltpu.VMEM((HEAD, 384), BF16),
            pltpu.VMEM((2, RT, HEAD), BF16),
            pltpu.VMEM((2, RT, HEAD), BF16),
            pltpu.VMEM((2, GRAD, HEAD), BF16),
            pltpu.VMEM((2, GRAD, HEAD), BF16),
            dma((80,)),
            dma((5,)),
            dma((2,)),
            dma((2, 2, 4)),
            dma((2, 2, 4)),
            dma((2,)),
            dma((4, 2)),
            dma((4, 2)),
            dma((2, 4, 2)),
            dma((2, 4, 2)),
            dma((2, 4, 2)),
            dma((2, 4, 2)),
            dma((2,)),
            dma((2,)),
            dma((2,)),
        ],
        compiler_params=pltpu.CompilerParams(
            collective_id=0, has_side_effects=True, vmem_limit_bytes=64 * 1024 * 1024
        ),
        name="attention_backward",
    )(line2, line3, q2, k2, v2, cot2.T, q3, k3, v3, cot3, weight)
    wide = jax.ShapeDtypeStruct((R2, 2 * HEAD), BF16)
    narrow = jax.ShapeDtypeStruct((R3, 2 * HEAD), BF16)
    return pl.pallas_call(
        lay_out,
        out_shape=(wide, wide, wide, narrow, narrow, narrow),
        in_specs=[vmem] * 2,
        out_specs=(hbm,) * 6,
        scratch_shapes=[dma((12,))],
        name="lay_out",
    )(*got)


def solution(mesh):
    shard = P("seq", "tp")
    in_specs = (shard, shard, shard, shard, P("seq"), shard, shard, shard, shard, P("seq"), P("tp", None))
    return jax.shard_map(on_device, mesh=mesh, in_specs=in_specs, out_specs=(shard,) * 6, check_vma=False)
```

```python
import functools
import math

import jax
import jax.numpy as jnp
from jax import lax
from jax.experimental import pallas as pl
from jax.experimental.pallas import tpu as pltpu
from jax.sharding import PartitionSpec as P

MESH = pl.DeviceIdType.MESH
F32, BF16 = jnp.float32, jnp.bfloat16
HEAD = 128
R2, R3 = 128, 64
RT = R2 + R3
FEAT = 320
NEG = -1e30
SCALE = 1.0 / math.sqrt(HEAD)
SCALE_TWO = SCALE * math.log2(math.e)
SLOT = 2 * RT + 16
GRAD = 2 * RT


def dot_nt(a, b):
    return lax.dot_general(a, b, (((1,), (1,)), ((), ())), preferred_element_type=F32)


def dot_nn(a, b):
    return lax.dot_general(a, b, (((1,), (0,)), ((), ())), preferred_element_type=F32)


def dot_tn(a, b):
    return lax.dot_general(a, b, (((0,), (0,)), ((), ())), preferred_element_type=F32)


def device(y, z, zh, x, c):
    return (y * 4 + z, (zh * 4 + x) * 2 + c)


def body(
    kept2, kept3, q2, k2, v2, cot2, q3, k3, v3, cot3, weight,
    dq_got, back_got,
    ct2, ct3, line2, line3, wv, kv, qb2, qb3, qt2, qt3, ob2, ob3, bias, outer2, outer3, ost2, ost3, acc2, acc3, st2, st3,
    stat, stat_out, stat_in, rb, sb, tmp, dqt2, dqt3, dqx_out, dqx_in, dq_out, dq_in, back_out, back_in,
    ssem, lsem, cot_z, cot_x, cot_s, kvin, qin, oin, ring, red, ring_s, red_s, xsem, backsem, dqsem,
):
    s, t = lax.axis_index("seq"), lax.axis_index("tp")
    y, z = lax.div(s, 4), lax.rem(s, 4)
    zh, x, c = lax.div(t, 8), lax.rem(lax.div(t, 2), 4), lax.rem(t, 2)
    zhalf, zpar = lax.div(z, 2), lax.rem(z, 2)

    sent = []

    def send(src, dst, sem, to, when=None):
        copy = pltpu.make_async_remote_copy(
            src_ref=src, dst_ref=dst, send_sem=ssem.at[len(sent)], recv_sem=sem,
            device_id=to, device_id_type=MESH,
        )
        if when is None:
            copy.start()
        else:
            pl.when(when)(copy.start)
        sent.append((copy, when))

    def keep(src, dst, sem, when=None):
        copy = pltpu.make_async_copy(src, dst, sem)
        if when is None:
            copy.start()
        else:
            pl.when(when)(copy.start)

    def arrive(ref, sem):
        pltpu.make_async_copy(ref, ref, sem).wait()

    def ct2_at(zz, xx, cc):
        return ct2.at[zz, xx, pl.ds(pl.multiple_of(cc * FEAT, 64), FEAT)]

    sibling = device(y, z, zh, x, 1 - c)
    y_up, y_down = lax.rem(y + 1, 8), lax.rem(y + 7, 8)

    barrier = pltpu.get_barrier_semaphore()
    peers = [device(y_up, z, zh, x, c), device(y_down, z, zh, x, c), device(y, z, 1 - zh, x, c), sibling]
    for dx in (1, 2, 3):
        peers.append(device(y, z, zh, lax.rem(x + dx, 4), c))
        for cc in (0, 1):
            peers.append(device(y, lax.rem(z + dx, 4), zh, x, cc))
    for peer in peers:
        pl.semaphore_signal(barrier, inc=1, device_id=peer, device_id_type=MESH)
    keep(kept2, line2, lsem.at[3])
    keep(kept3, line3, lsem.at[4])
    keep(cot2, ct2_at(zh, x, c), lsem.at[0])
    keep(cot3, ct3.at[zh, x, c], lsem.at[1])
    keep(weight, wv, lsem.at[2])
    pl.semaphore_wait(barrier, len(peers))

    def clear():
        stat[...] = jnp.where(lax.broadcasted_iota(jnp.int32, stat.shape, 0) == 0, NEG, 0.0)
        for ref in (acc2, acc3, dqt2, dqt3, outer2, outer3):
            ref[...] = jnp.zeros_like(ref)

    far = device(y, z, 1 - zh, x, c)
    mine2, mine3 = ct2_at(zh, x, c), ct3.at[zh, x, c]
    def cot_far():
        send(cot2, mine2, cot_z.at[0], far)
        send(cot3, mine3, cot_z.at[1], far)

    def make_bias():
        arrive(line2, lsem.at[3])
        arrive(line3, lsem.at[4])
        rows = lax.broadcasted_iota(jnp.int32, (16, HEAD), 0)
        live2 = jnp.where(line2[...] >= 0, 0.0, NEG)
        live3 = jnp.where(line3[...] >= 0, 0.0, NEG)
        live3 = jnp.concatenate([live3, live3], axis=1)
        bias[...] = jnp.where(rows == 0, live2, jnp.where(rows == 1, live3, 0.0)).astype(BF16)

    def keys_send():
        slot = kv.at[y, zpar]
        sem = kvin.at[zpar]

        def each(parts):
            for hh in (0, 1):
                here = (zhalf == c) & (zpar == hh)
                away = jnp.logical_not(here)
                to = device(y, 2 * c + hh, zh, x, zhalf)
                for src, dst in parts(pl.ds(hh * HEAD, HEAD)):
                    keep(src, dst, sem, here)
                    send(src, dst, sem, to, away)

        each(lambda cols: (
            (k2.at[:, cols], slot.at[0:R2]),
            (k3.at[:, cols], slot.at[R2:RT]),
            (v2.at[:, cols], slot.at[RT:RT + R2]),
            (v3.at[:, cols], slot.at[RT + R2:GRAD]),
        ))
        make_bias()
        each(lambda cols: ((bias, slot.at[GRAD:SLOT]),))

    def cot_near():
        for dx in (1, 3, 2):
            to = device(y, z, zh, lax.rem(x + dx, 4), c)
            send(cot2, mine2, cot_x.at[0, 0, x], to)
            send(cot3, mine3, cot_x.at[1, 0, x], to)
        send(cot2, mine2, cot_s.at[0, zh, x], sibling)
        send(cot3, mine3, cot_s.at[1, zh, x], sibling)

    def cot_arrive(zz, xx, kind):
        for depth, ref in enumerate((ct2_at(zz, xx, c), ct3.at[zz, xx, c])):
            arrive(ref, cot_x.at[depth, kind, xx])
            send(ref, ref, cot_s.at[depth, zz, xx], sibling)

    def rows2(zz):
        return pl.ds(pl.multiple_of(zz * R2, R2), R2)

    def rows3(zz):
        return pl.ds(pl.multiple_of(zz * R3, R3), R3)

    def to_workers(hh, parts, places, sems):
        here = (zhalf == c) & (zpar == hh)
        away = jnp.logical_not(here)
        to = device(y, 2 * c + hh, zh, x, zhalf)
        for depth, (src, dst) in enumerate(zip(parts, places(z))):
            keep(src, dst, sems.at[z, depth], here)
            send(src, dst, sems.at[z, depth], to, away)

    def hand_on(places, sems):
        for k in (0, 1):
            for depth, ref in enumerate(places(2 * c + k)):
                sem = sems.at[2 * c + k, depth]
                arrive(ref, sem)
                send(ref, ref, sem, sibling)

    def handed(places, sems):
        for k in (0, 1):
            for depth, ref in enumerate(places(2 * (1 - c) + k)):
                arrive(ref, sems.at[2 * (1 - c) + k, depth])

    def query_places(zz):
        return qb2.at[rows2(zz)], qb3.at[rows3(zz)]

    def outer_places(zz):
        return ob2.at[:, rows2(zz)], ob3.at[rows3(zz)]

    def queries_send():
        for hh in (0, 1):
            cols = pl.ds(hh * HEAD, HEAD)
            to_workers(hh, (q2.at[:, cols], q3.at[:, cols]), query_places, qin)

    ring_to = (device(y_up, z, zh, x, c), device(y_down, z, zh, x, c))

    def origin(direction, step):
        return lax.rem(y + (8 - step if direction == 0 else step), 8)

    ring_sent = []

    def ring_send(direction, step, sub, at):
        slot = kv.at[at, sub]
        copy = pltpu.make_async_remote_copy(
            src_ref=slot, dst_ref=slot, send_sem=ring_s.at[direction, step, sub], recv_sem=ring.at[direction, step, sub],
            device_id=ring_to[direction], device_id_type=MESH,
        )
        copy.start()
        ring_sent.append(copy)

    def ring_step(step):
        for sub in (0, 1):
            for direction in (0, 1):
                if step == 4 and sub != direction:
                    continue
                at = origin(direction, step)
                arrive(kv.at[at, sub], ring.at[direction, step - 1, sub])
                if step < 3 or (step == 3 and sub == direction):
                    ring_send(direction, step, sub, at)

    row2 = pl.ds(0, 512)
    row3 = pl.ds(512, 256)

    def both(at, rows):
        return jnp.concatenate([kv[at, 0, rows], kv[at, 1, rows]], axis=0)

    def early_part(at, rows_k, rows_v, queries, column, row, store, acc, first):
        scores = dot_nn(both(at, rows_k), queries[...]) * SCALE_TWO + column
        if first is not None:
            key_slot = lax.broadcasted_iota(jnp.int32, scores.shape, 0) + first
            query_slot = lax.broadcasted_iota(jnp.int32, scores.shape, 1)
            scores = jnp.where(key_slot <= query_slot, scores, NEG)
        store[at] = scores
        before = stat[0:1, row]
        now = jnp.maximum(before, jnp.max(scores, axis=0, keepdims=True))
        weights = jnp.exp2(scores - now)
        fade = jnp.exp2(before - now)
        stat[0:1, row] = now
        stat[1:2, row] = stat[1:2, row] * fade + jnp.sum(weights, axis=0, keepdims=True)
        acc[...] = acc[...] * fade + dot_tn(both(at, rows_v), weights.astype(BF16))

    def early_now(at, own):
        lines = [kv[at, sub, GRAD:SLOT].astype(F32) for sub in (0, 1)]
        turned = jnp.concatenate(lines + [jnp.zeros((HEAD - 32, HEAD), F32)], axis=0).T
        column2 = jnp.concatenate([turned[:, 0:1], turned[:, 16:17]], axis=0)
        column3 = jnp.concatenate([turned[0:R3, 1:2], turned[0:R3, 17:18]], axis=0)
        early_part(at, pl.ds(0, R2), pl.ds(RT, R2), qt2, column2, row2, st2, acc2, 2 * R2 * c if own else None)
        early_part(at, pl.ds(R2, R3), pl.ds(RT + R2, R3), qt3, column3, row3, st3, acc3, 2 * R3 * c if own else None)

    def early_step(step):
        if step == 0:
            early_now(y, True)
            return

        @pl.loop(0, 1 if step == 4 else 2)
        def _(forward):
            at = lax.rem(y + 8 + (2 * forward - 1) * step, 8)

            @pl.when(at < y)
            def _():
                early_now(at, False)

    def own_keys():
        arrive(kv.at[y, 0], kvin.at[0])
        arrive(kv.at[y, 1], kvin.at[1])
        for sub in (0, 1):
            for direction in (0, 1):
                ring_send(direction, 0, sub, y)

    def near_shards():
        for dx in (1, 3, 2):
            cot_arrive(zh, lax.rem(x + dx, 4), 0)

    def queries_over():
        hand_on(query_places, qin)

    def queries_here():
        handed(query_places, qin)
        qt2[...] = qb2[...].T
        qt3[...] = qb3[...].T

    def far_shard(depth):
        other = (ct2_at(1 - zh, x, c), ct3.at[1 - zh, x, c])[depth]
        arrive(other, cot_z.at[depth])
        for dx in (1, 3, 2):
            to = device(y, z, zh, lax.rem(x + dx, 4), c)
            send(other, other, cot_x.at[depth, 1, x], to)
        send(other, other, cot_s.at[depth, 1 - zh, x], sibling)

    def far_near_shards():
        for dx in (1, 3, 2):
            cot_arrive(1 - zh, lax.rem(x + dx, 4), 1)

    def project(zz):
        totals = [outer2[...], outer3[...]]
        for xx in range(4):
            part = wv[:, pl.ds(pl.multiple_of((zz * 4 + xx) * 2 * FEAT, HEAD), 2 * FEAT)]
            features = jnp.concatenate([ct3[zz, xx, 0], ct3[zz, xx, 1]], axis=1)
            totals[0] += dot_nn(part, ct2[zz, xx])
            totals[1] += dot_nt(part, features)
        outer2[...], outer3[...] = totals

    def sibling_shards(zz):
        for xx in range(4):
            arrive(ct2_at(zz, xx, 1 - c), cot_s.at[0, zz, xx])
            arrive(ct3.at[zz, xx, 1 - c], cot_s.at[1, zz, xx])

    def near_project():
        arrive(mine2, lsem.at[0])
        arrive(mine3, lsem.at[1])
        arrive(wv, lsem.at[2])
        sibling_shards(zh)
        project(zh)

    def far_project():
        sibling_shards(1 - zh)
        project(1 - zh)

    def outer_send():
        lines = bias[...].astype(F32)
        dead = jnp.concatenate([lines, jnp.zeros((HEAD - 16, HEAD), F32)], axis=0).T[0:R3, 1:2]
        part2 = jnp.where(lines[0:1] < 0.0, 0.0, outer2[...]).astype(BF16)
        part3 = jnp.where(dead < 0.0, 0.0, outer3[...].T).astype(BF16)
        for hh in (0, 1):
            ost2[hh] = part2[hh * HEAD:(hh + 1) * HEAD]
            ost3[hh] = part3[:, hh * HEAD:(hh + 1) * HEAD]
            to_workers(hh, (ost2.at[hh], ost3.at[hh]), outer_places, oin)

    def outer_over():
        hand_on(outer_places, oin)

    def outer_here():
        handed(outer_places, oin)

    keys_send()
    cot_far()
    cot_near()
    clear()
    own_keys()
    near_shards()
    queries_send()
    ring_step(1)
    far_shard(0)
    far_shard(1)
    queries_over()
    queries_here()
    early_step(0)
    ring_step(2)
    near_project()
    early_step(1)
    far_near_shards()
    ring_step(3)
    far_project()
    outer_send()
    early_step(2)
    early_step(3)
    ring_step(4)
    outer_over()
    early_step(4)
    outer_here()

    stat_out[...] = stat[...]
    stat_out[2:3, row2] = jnp.sum(ob2[...].astype(F32) * acc2[...], axis=0, keepdims=True)
    stat_out[2:3, row3] = jnp.sum(ob3[...].astype(F32).T * acc3[...], axis=0, keepdims=True)
    send(stat_out, stat_in, xsem.at[0], sibling)
    arrive(stat_in, xsem.at[0])
    top = jnp.maximum(stat_out[0:1], stat_in[0:1])
    own_part, other_part = jnp.exp2(stat_out[0:1] - top), jnp.exp2(stat_in[0:1] - top)
    total = stat_out[1:2] * own_part + stat_in[1:2] * other_part
    stat[3:4] = top + jnp.log2(total)
    stat[4:5] = (stat_out[2:3] * own_part + stat_in[2:3] * other_part) / total

    def late_part(at, side, rows_k, rows_v, queries, outers, row, store, dqt, by_rows, by_columns):
        probability = jnp.exp2(store[at] - stat[3:4, row])
        grad_probs = by_rows(both(at, rows_v), outers[...])
        grad_low = (probability * (grad_probs - stat[4:5, row])).astype(BF16)
        keys = dot_nn(grad_low, queries[...]) * SCALE
        values = by_columns(probability.astype(BF16), outers[...])
        count = keys.shape[0] // 2
        for sub in (0, 1):
            tmp[side, sub, rows_k] = keys[sub * count:(sub + 1) * count]
            tmp[side, sub, rows_v] = values[sub * count:(sub + 1) * count]
        half = grad_low.shape[1] // 2
        for h in (0, 1):
            dqt[h] += dot_tn(both(at, rows_k), grad_low[:, h * half:(h + 1) * half])

    def late_now(at, side):
        late_part(at, side, pl.ds(0, R2), pl.ds(RT, R2), qb2, ob2, row2, st2, dqt2, dot_nn, dot_nt)
        late_part(at, side, pl.ds(R2, R3), pl.ds(RT + R2, R3), qb3, ob3, row3, st3, dqt3, dot_nt, dot_nn)

    def late(at, side):
        @pl.when(at < y)
        def _():
            late_now(at, side)

        @pl.when(at > y)
        def _():
            tmp[side] = jnp.zeros((2, GRAD, HEAD), F32)

    def red_copy(direction, step, sub, part):
        rows = pl.ds(part * RT, RT)
        return pltpu.make_async_remote_copy(
            src_ref=sb.at[direction, step, sub, rows], dst_ref=rb.at[direction, step, sub, rows],
            send_sem=red_s.at[direction, step, sub, part], recv_sem=red.at[direction, step, sub, part],
            device_id=ring_to[direction], device_id_type=MESH,
        )

    def red_here(direction, step, sub, part):
        rows = pl.ds(part * RT, RT)
        arrive(rb.at[direction, step, sub, rows], red.at[direction, step, sub, part])
        return rb[direction, step, sub, rows].astype(F32)

    def red_send(direction, step, sub, add, side):
        for part in (0, 1):
            rows = pl.ds(part * RT, RT)
            value = tmp[side, sub, rows]
            if add:
                value = value + red_here(direction, step - 1, sub, part)
            sb[direction, step, sub, rows] = value.astype(BF16)
            red_copy(direction, step, sub, part).start()

    red_order = ((0, 1), (1, 0), (0, 0), (1, 1))
    late(lax.rem(y + 4, 8), 0)
    for sub in (0, 1):
        red_send(sub, 0, sub, False, 0)
    for step in (1, 2, 3):

        @pl.loop(0, 2)
        def _(side):
            late(lax.rem(y + (4 - step) + side * 2 * (4 + step), 8), side)

        for direction, sub in red_order:
            red_send(direction, step, sub, step > 1 or direction == sub, direction)

    late_now(y, 0)

    dqx_out[:, 0:256] = dqt2[1 - c].astype(BF16)
    dqx_out[:, 256:384] = dqt3[1 - c].astype(BF16)
    send(dqx_out, dqx_in, xsem.at[1], sibling)
    arrive(dqx_in, xsem.at[1])
    query_two = (dqt2[c] + dqx_in[:, 0:256].astype(F32)) * SCALE
    query_three = (dqt3[c] + dqx_in[:, 256:384].astype(F32)) * SCALE
    rows_two, rows_three = query_two.T.astype(BF16), query_three.T.astype(BF16)

    def to_source(src, dst, sem, sub):
        to = device(y, 2 * c + sub, zh, x, zhalf)
        here = (z == 2 * c + sub) & (zhalf == c)
        keep(src, dst, sem, here)
        send(src, dst, sem, to, jnp.logical_not(here))

    for sub in (0, 1):
        dq_out[sub, 0:R2] = rows_two[sub * R2:(sub + 1) * R2]
        dq_out[sub, R2:RT] = rows_three[sub * R3:(sub + 1) * R3]
        to_source(dq_out.at[sub], dq_in.at[zpar], dqsem.at[zpar], sub)

    for part in (0, 1):
        rows = pl.ds(part * RT, RT)
        for sub in (0, 1):
            value = tmp[0, sub, rows]
            for direction in (sub, 1 - sub):
                value = value + red_here(direction, 3, sub, part)
            back_out[sub, rows] = value.astype(BF16)
            to_source(back_out.at[sub, rows], back_in.at[zpar, rows], backsem.at[zpar, part], sub)

    for hh in (0, 1):
        arrive(dq_in.at[hh], dqsem.at[hh])
    dq_got[...] = dq_in[...]
    for hh in (0, 1):
        for part in (0, 1):
            arrive(back_in.at[hh, pl.ds(part * RT, RT)], backsem.at[hh, part])
    back_got[...] = back_in[...]

    for copy, when in sent:
        if when is None:
            copy.wait_send()
        else:
            pl.when(when)(copy.wait_send)
    for copy in ring_sent:
        copy.wait_send()
    for step in range(4):
        for sub in (0, 1):
            for direction in (0, 1):
                if step > 0 or sub == direction:
                    for part in (0, 1):
                        red_copy(direction, step, sub, part).wait_send()


def lay_out(dq_got, back_got, dq2, dk2, dv2, dq3, dk3, dv3, sem):
    copies = []
    for hh in (0, 1):
        cols = pl.ds(hh * HEAD, HEAD)
        parts = (
            (back_got.at[hh, 0:R2], dk2),
            (back_got.at[hh, RT:RT + R2], dv2),
            (dq_got.at[hh, 0:R2], dq2),
            (back_got.at[hh, R2:RT], dk3),
            (back_got.at[hh, RT + R2:GRAD], dv3),
            (dq_got.at[hh, R2:RT], dq3),
        )
        for src, dst in parts:
            copies.append(pltpu.make_async_copy(src, dst.at[:, cols], sem.at[len(copies)]))
    for copy in copies:
        copy.start()
    for copy in copies:
        copy.wait()


def on_device(q2, k2, v2, cot2, kept2, q3, k3, v3, cot3, kept3, weight):
    hbm = pl.BlockSpec(memory_space=pltpu.HBM)
    vmem = pl.BlockSpec(memory_space=pltpu.VMEM)
    dma = pltpu.SemaphoreType.DMA
    line2 = kept2.reshape(1, R2)
    line3 = kept3.reshape(1, R3)
    got = pl.pallas_call(
        body,
        out_shape=(
            jax.ShapeDtypeStruct((2, RT, HEAD), BF16),
            jax.ShapeDtypeStruct((2, GRAD, HEAD), BF16),
        ),
        in_specs=[hbm] * 11,
        out_specs=(vmem,) * 2,
        scratch_shapes=[
            pltpu.VMEM((2, 4, 2 * FEAT, R2), BF16),
            pltpu.VMEM((2, 4, 2, R3, FEAT), BF16),
            pltpu.VMEM((1, R2), jnp.int32),
            pltpu.VMEM((1, R3), jnp.int32),
            pltpu.VMEM((2 * HEAD, 16 * FEAT), BF16),
            pltpu.VMEM((8, 2, SLOT, HEAD), BF16),
            pltpu.VMEM((512, HEAD), BF16),
            pltpu.VMEM((256, HEAD), BF16),
            pltpu.VMEM((HEAD, 512), BF16),
            pltpu.VMEM((HEAD, 256), BF16),
            pltpu.VMEM((HEAD, 512), BF16),
            pltpu.VMEM((256, HEAD), BF16),
            pltpu.VMEM((16, HEAD), BF16),
            pltpu.VMEM((2 * HEAD, R2), F32),
            pltpu.VMEM((2 * HEAD, R3), F32),
            pltpu.VMEM((2, HEAD, R2), BF16),
            pltpu.VMEM((2, R3, HEAD), BF16),
            pltpu.VMEM((HEAD, 512), F32),
            pltpu.VMEM((HEAD, 256), F32),
            pltpu.VMEM((8, 2 * R2, 512), F32),
            pltpu.VMEM((8, 2 * R3, 256), F32),
            pltpu.VMEM((8, 768), F32),
            pltpu.VMEM((8, 768), F32),
            pltpu.VMEM((8, 768), F32),
            pltpu.VMEM((2, 4, 2, GRAD, HEAD), BF16),
            pltpu.VMEM((2, 4, 2, GRAD, HEAD), BF16),
            pltpu.VMEM((2, 2, GRAD, HEAD), F32),
            pltpu.VMEM((2, HEAD, 256), F32),
            pltpu.VMEM((2, HEAD, 128), F32),
            pltpu.VMEM((HEAD, 384), BF16),
            pltpu.VMEM((HEAD, 384), BF16),
            pltpu.VMEM((2, RT, HEAD), BF16),
            pltpu.VMEM((2, RT, HEAD), BF16),
            pltpu.VMEM((2, GRAD, HEAD), BF16),
            pltpu.VMEM((2, GRAD, HEAD), BF16),
            dma((80,)),
            dma((5,)),
            dma((2,)),
            dma((2, 2, 4)),
            dma((2, 2, 4)),
            dma((2,)),
            dma((4, 2)),
            dma((4, 2)),
            dma((2, 4, 2)),
            dma((2, 4, 2, 2)),
            dma((2, 4, 2)),
            dma((2, 4, 2, 2)),
            dma((2,)),
            dma((2, 2)),
            dma((2,)),
        ],
        compiler_params=pltpu.CompilerParams(
            collective_id=0, has_side_effects=True, vmem_limit_bytes=64 * 1024 * 1024
        ),
        name="attention_backward",
    )(line2, line3, q2, k2, v2, cot2.T, q3, k3, v3, cot3, weight)
    wide = jax.ShapeDtypeStruct((R2, 2 * HEAD), BF16)
    narrow = jax.ShapeDtypeStruct((R3, 2 * HEAD), BF16)
    return pl.pallas_call(
        lay_out,
        out_shape=(wide, wide, wide, narrow, narrow, narrow),
        in_specs=[vmem] * 2,
        out_specs=(hbm,) * 6,
        scratch_shapes=[dma((12,))],
        name="lay_out",
    )(*got)


def solution(mesh):
    shard = P("seq", "tp")
    in_specs = (shard, shard, shard, shard, P("seq"), shard, shard, shard, shard, P("seq"), P("tp", None))
    return jax.shard_map(on_device, mesh=mesh, in_specs=in_specs, out_specs=(shard,) * 6, check_vma=False)
```

```python
import functools
import math

import jax
import jax.numpy as jnp
from jax import lax
from jax.experimental import pallas as pl
from jax.experimental.pallas import tpu as pltpu
from jax.sharding import PartitionSpec as P

MESH = pl.DeviceIdType.MESH
F32, BF16 = jnp.float32, jnp.bfloat16
HEAD = 128
R2, R3 = 128, 64
RT = R2 + R3
FEAT = 320
NEG = -1e30
SCALE = 1.0 / math.sqrt(HEAD)
SCALE_TWO = SCALE * math.log2(math.e)
SLOT = 2 * RT + 16
GRAD = 2 * RT


def dot_nt(a, b):
    return lax.dot_general(a, b, (((1,), (1,)), ((), ())), preferred_element_type=F32)


def dot_nn(a, b):
    return lax.dot_general(a, b, (((1,), (0,)), ((), ())), preferred_element_type=F32)


def dot_tn(a, b):
    return lax.dot_general(a, b, (((0,), (0,)), ((), ())), preferred_element_type=F32)


def device(y, z, zh, x, c):
    return (y * 4 + z, (zh * 4 + x) * 2 + c)


def body(
    kept2, kept3, q2, k2, v2, cot2, q3, k3, v3, cot3, weight,
    dq_got, back_got,
    ct2, ct3, line2, line3, wv, kv, qb2, qb3, qt2, qt3, ob2, ob3, bias, outer2, outer3, ost2, ost3, acc2, acc3, st2, st3,
    stat, stat_out, stat_in, rb, sb, tmp, dqt2, dqt3, dqx_out, dqx_in, dq_out, dq_in, back_out, back_in,
    ssem, lsem, cot_z, cot_x, cot_s, kvin, qin, oin, ring, red, ring_s, red_s, xsem, backsem, dqsem, outsem,
):
    s, t = lax.axis_index("seq"), lax.axis_index("tp")
    y, z = lax.div(s, 4), lax.rem(s, 4)
    zh, x, c = lax.div(t, 8), lax.rem(lax.div(t, 2), 4), lax.rem(t, 2)
    zhalf, zpar = lax.div(z, 2), lax.rem(z, 2)

    sent = []

    def send(src, dst, sem, to, when=None):
        copy = pltpu.make_async_remote_copy(
            src_ref=src, dst_ref=dst, send_sem=ssem.at[len(sent)], recv_sem=sem,
            device_id=to, device_id_type=MESH,
        )
        if when is None:
            copy.start()
        else:
            pl.when(when)(copy.start)
        sent.append((copy, when))

    def keep(src, dst, sem, when=None):
        copy = pltpu.make_async_copy(src, dst, sem)
        if when is None:
            copy.start()
        else:
            pl.when(when)(copy.start)

    def arrive(ref, sem):
        pltpu.make_async_copy(ref, ref, sem).wait()

    def ct2_at(zz, xx, cc):
        return ct2.at[zz, xx, pl.ds(pl.multiple_of(cc * FEAT, 64), FEAT)]

    sibling = device(y, z, zh, x, 1 - c)
    y_up, y_down = lax.rem(y + 1, 8), lax.rem(y + 7, 8)

    barrier = pltpu.get_barrier_semaphore()
    peers = [device(y_up, z, zh, x, c), device(y_down, z, zh, x, c), device(y, z, 1 - zh, x, c), sibling]
    for dx in (1, 2, 3):
        peers.append(device(y, z, zh, lax.rem(x + dx, 4), c))
        for cc in (0, 1):
            peers.append(device(y, lax.rem(z + dx, 4), zh, x, cc))
    for peer in peers:
        pl.semaphore_signal(barrier, inc=1, device_id=peer, device_id_type=MESH)
    keep(kept2, line2, lsem.at[3])
    keep(kept3, line3, lsem.at[4])
    keep(cot2, ct2_at(zh, x, c), lsem.at[0])
    keep(cot3, ct3.at[zh, x, c], lsem.at[1])
    keep(weight, wv, lsem.at[2])
    pl.semaphore_wait(barrier, len(peers))

    def clear():
        stat[...] = jnp.where(lax.broadcasted_iota(jnp.int32, stat.shape, 0) == 0, NEG, 0.0)
        for ref in (acc2, acc3, dqt2, dqt3, outer2, outer3):
            ref[...] = jnp.zeros_like(ref)

    far = device(y, z, 1 - zh, x, c)
    mine2, mine3 = ct2_at(zh, x, c), ct3.at[zh, x, c]
    def cot_far():
        send(cot2, mine2, cot_z.at[0], far)
        send(cot3, mine3, cot_z.at[1], far)

    def make_bias():
        arrive(line2, lsem.at[3])
        arrive(line3, lsem.at[4])
        rows = lax.broadcasted_iota(jnp.int32, (16, HEAD), 0)
        live2 = jnp.where(line2[...] >= 0, 0.0, NEG)
        live3 = jnp.where(line3[...] >= 0, 0.0, NEG)
        live3 = jnp.concatenate([live3, live3], axis=1)
        bias[...] = jnp.where(rows == 0, live2, jnp.where(rows == 1, live3, 0.0)).astype(BF16)

    def keys_send():
        slot = kv.at[y, zpar]
        sem = kvin.at[zpar]

        def each(parts):
            for hh in (0, 1):
                here = (zhalf == c) & (zpar == hh)
                away = jnp.logical_not(here)
                to = device(y, 2 * c + hh, zh, x, zhalf)
                for src, dst in parts(pl.ds(hh * HEAD, HEAD)):
                    keep(src, dst, sem, here)
                    send(src, dst, sem, to, away)

        each(lambda cols: (
            (k2.at[:, cols], slot.at[0:R2]),
            (k3.at[:, cols], slot.at[R2:RT]),
            (v2.at[:, cols], slot.at[RT:RT + R2]),
            (v3.at[:, cols], slot.at[RT + R2:GRAD]),
        ))
        make_bias()
        each(lambda cols: ((bias, slot.at[GRAD:SLOT]),))

    def cot_near():
        for dx in (1, 3, 2):
            to = device(y, z, zh, lax.rem(x + dx, 4), c)
            send(cot2, mine2, cot_x.at[0, 0, x], to)
            send(cot3, mine3, cot_x.at[1, 0, x], to)
        send(cot2, mine2, cot_s.at[0, zh, x], sibling)
        send(cot3, mine3, cot_s.at[1, zh, x], sibling)

    def cot_arrive(zz, xx, kind):
        for depth, ref in enumerate((ct2_at(zz, xx, c), ct3.at[zz, xx, c])):
            arrive(ref, cot_x.at[depth, kind, xx])
            send(ref, ref, cot_s.at[depth, zz, xx], sibling)

    def rows2(zz):
        return pl.ds(pl.multiple_of(zz * R2, R2), R2)

    def rows3(zz):
        return pl.ds(pl.multiple_of(zz * R3, R3), R3)

    def to_workers(hh, parts, places, sems):
        here = (zhalf == c) & (zpar == hh)
        away = jnp.logical_not(here)
        to = device(y, 2 * c + hh, zh, x, zhalf)
        for depth, (src, dst) in enumerate(zip(parts, places(z))):
            keep(src, dst, sems.at[z, depth], here)
            send(src, dst, sems.at[z, depth], to, away)

    def hand_on(places, sems):
        for k in (0, 1):
            for depth, ref in enumerate(places(2 * c + k)):
                sem = sems.at[2 * c + k, depth]
                arrive(ref, sem)
                send(ref, ref, sem, sibling)

    def handed(places, sems):
        for k in (0, 1):
            for depth, ref in enumerate(places(2 * (1 - c) + k)):
                arrive(ref, sems.at[2 * (1 - c) + k, depth])

    def query_places(zz):
        return qb2.at[rows2(zz)], qb3.at[rows3(zz)]

    def outer_places(zz):
        return ob2.at[:, rows2(zz)], ob3.at[rows3(zz)]

    def queries_send():
        for hh in (0, 1):
            cols = pl.ds(hh * HEAD, HEAD)
            to_workers(hh, (q2.at[:, cols], q3.at[:, cols]), query_places, qin)

    ring_to = (device(y_up, z, zh, x, c), device(y_down, z, zh, x, c))

    def origin(direction, step):
        return lax.rem(y + (8 - step if direction == 0 else step), 8)

    ring_sent = []

    def ring_send(direction, step, sub, at):
        slot = kv.at[at, sub]
        copy = pltpu.make_async_remote_copy(
            src_ref=slot, dst_ref=slot, send_sem=ring_s.at[direction, step, sub], recv_sem=ring.at[direction, step, sub],
            device_id=ring_to[direction], device_id_type=MESH,
        )
        copy.start()
        ring_sent.append(copy)

    def ring_step(step):
        for sub in (0, 1):
            for direction in (0, 1):
                if step == 4 and sub != direction:
                    continue
                at = origin(direction, step)
                arrive(kv.at[at, sub], ring.at[direction, step - 1, sub])
                if step < 3 or (step == 3 and sub == direction):
                    ring_send(direction, step, sub, at)

    row2 = pl.ds(0, 512)
    row3 = pl.ds(512, 256)

    def both(at, rows):
        return jnp.concatenate([kv[at, 0, rows], kv[at, 1, rows]], axis=0)

    def early_part(at, rows_k, rows_v, queries, column, row, store, acc, first):
        scores = dot_nn(both(at, rows_k), queries[...]) * SCALE_TWO + column
        if first is not None:
            key_slot = lax.broadcasted_iota(jnp.int32, scores.shape, 0) + first
            query_slot = lax.broadcasted_iota(jnp.int32, scores.shape, 1)
            scores = jnp.where(key_slot <= query_slot, scores, NEG)
        store[at] = scores
        before = stat[0:1, row]
        now = jnp.maximum(before, jnp.max(scores, axis=0, keepdims=True))
        weights = jnp.exp2(scores - now)
        fade = jnp.exp2(before - now)
        stat[0:1, row] = now
        stat[1:2, row] = stat[1:2, row] * fade + jnp.sum(weights, axis=0, keepdims=True)
        acc[...] = acc[...] * fade + dot_tn(both(at, rows_v), weights.astype(BF16))

    def early_now(at, own):
        lines = [kv[at, sub, GRAD:SLOT].astype(F32) for sub in (0, 1)]
        turned = jnp.concatenate(lines + [jnp.zeros((HEAD - 32, HEAD), F32)], axis=0).T
        column2 = jnp.concatenate([turned[:, 0:1], turned[:, 16:17]], axis=0)
        column3 = jnp.concatenate([turned[0:R3, 1:2], turned[0:R3, 17:18]], axis=0)
        early_part(at, pl.ds(0, R2), pl.ds(RT, R2), qt2, column2, row2, st2, acc2, 2 * R2 * c if own else None)
        early_part(at, pl.ds(R2, R3), pl.ds(RT + R2, R3), qt3, column3, row3, st3, acc3, 2 * R3 * c if own else None)

    def early_step(step):
        if step == 0:
            early_now(y, True)
            return

        @pl.loop(0, 1 if step == 4 else 2)
        def _(forward):
            at = lax.rem(y + 8 + (2 * forward - 1) * step, 8)

            @pl.when(at < y)
            def _():
                early_now(at, False)

    def own_keys():
        arrive(kv.at[y, 0], kvin.at[0])
        arrive(kv.at[y, 1], kvin.at[1])
        for sub in (0, 1):
            for direction in (0, 1):
                ring_send(direction, 0, sub, y)

    def near_shards():
        for dx in (1, 3, 2):
            cot_arrive(zh, lax.rem(x + dx, 4), 0)

    def queries_over():
        hand_on(query_places, qin)

    def queries_here():
        handed(query_places, qin)
        qt2[...] = qb2[...].T
        qt3[...] = qb3[...].T

    def far_shard(depth):
        other = (ct2_at(1 - zh, x, c), ct3.at[1 - zh, x, c])[depth]
        arrive(other, cot_z.at[depth])
        for dx in (1, 3, 2):
            to = device(y, z, zh, lax.rem(x + dx, 4), c)
            send(other, other, cot_x.at[depth, 1, x], to)
        send(other, other, cot_s.at[depth, 1 - zh, x], sibling)

    def far_near_shards():
        for dx in (1, 3, 2):
            cot_arrive(1 - zh, lax.rem(x + dx, 4), 1)

    def project(zz):
        totals = [outer2[...], outer3[...]]
        for xx in range(4):
            part = wv[:, pl.ds(pl.multiple_of((zz * 4 + xx) * 2 * FEAT, HEAD), 2 * FEAT)]
            features = jnp.concatenate([ct3[zz, xx, 0], ct3[zz, xx, 1]], axis=1)
            totals[0] += dot_nn(part, ct2[zz, xx])
            totals[1] += dot_nt(part, features)
        outer2[...], outer3[...] = totals

    def sibling_shards(zz):
        for xx in range(4):
            arrive(ct2_at(zz, xx, 1 - c), cot_s.at[0, zz, xx])
            arrive(ct3.at[zz, xx, 1 - c], cot_s.at[1, zz, xx])

    def near_project():
        arrive(mine2, lsem.at[0])
        arrive(mine3, lsem.at[1])
        arrive(wv, lsem.at[2])
        sibling_shards(zh)
        project(zh)

    def far_project():
        sibling_shards(1 - zh)
        project(1 - zh)

    def outer_send():
        lines = bias[...].astype(F32)
        dead = jnp.concatenate([lines, jnp.zeros((HEAD - 16, HEAD), F32)], axis=0).T[0:R3, 1:2]
        part2 = jnp.where(lines[0:1] < 0.0, 0.0, outer2[...]).astype(BF16)
        part3 = jnp.where(dead < 0.0, 0.0, outer3[...].T).astype(BF16)
        for hh in (0, 1):
            ost2[hh] = part2[hh * HEAD:(hh + 1) * HEAD]
            ost3[hh] = part3[:, hh * HEAD:(hh + 1) * HEAD]
            to_workers(hh, (ost2.at[hh], ost3.at[hh]), outer_places, oin)

    def outer_over():
        hand_on(outer_places, oin)

    def outer_here():
        handed(outer_places, oin)

    keys_send()
    cot_far()
    cot_near()
    clear()
    own_keys()
    near_shards()
    queries_send()
    ring_step(1)
    far_shard(0)
    far_shard(1)
    queries_over()
    queries_here()
    early_step(0)
    ring_step(2)
    near_project()
    early_step(1)
    far_near_shards()
    ring_step(3)
    far_project()
    outer_send()
    early_step(2)
    early_step(3)
    ring_step(4)
    outer_over()
    early_step(4)
    outer_here()

    stat_out[...] = stat[...]
    stat_out[2:3, row2] = jnp.sum(ob2[...].astype(F32) * acc2[...], axis=0, keepdims=True)
    stat_out[2:3, row3] = jnp.sum(ob3[...].astype(F32).T * acc3[...], axis=0, keepdims=True)
    send(stat_out, stat_in, xsem.at[0], sibling)
    arrive(stat_in, xsem.at[0])
    top = jnp.maximum(stat_out[0:1], stat_in[0:1])
    own_part, other_part = jnp.exp2(stat_out[0:1] - top), jnp.exp2(stat_in[0:1] - top)
    total = stat_out[1:2] * own_part + stat_in[1:2] * other_part
    stat[3:4] = top + jnp.log2(total)
    stat[4:5] = (stat_out[2:3] * own_part + stat_in[2:3] * other_part) / total

    def late_part(at, side, rows_k, rows_v, queries, outers, row, store, dqt, by_rows, by_columns):
        probability = jnp.exp2(store[at] - stat[3:4, row])
        grad_probs = by_rows(both(at, rows_v), outers[...])
        grad_low = (probability * (grad_probs - stat[4:5, row])).astype(BF16)
        keys = dot_nn(grad_low, queries[...]) * SCALE
        values = by_columns(probability.astype(BF16), outers[...])
        count = keys.shape[0] // 2
        for sub in (0, 1):
            tmp[side, sub, rows_k] = keys[sub * count:(sub + 1) * count]
            tmp[side, sub, rows_v] = values[sub * count:(sub + 1) * count]
        half = grad_low.shape[1] // 2
        for h in (0, 1):
            dqt[h] += dot_tn(both(at, rows_k), grad_low[:, h * half:(h + 1) * half])

    def late_now(at, side):
        late_part(at, side, pl.ds(0, R2), pl.ds(RT, R2), qb2, ob2, row2, st2, dqt2, dot_nn, dot_nt)
        late_part(at, side, pl.ds(R2, R3), pl.ds(RT + R2, R3), qb3, ob3, row3, st3, dqt3, dot_nt, dot_nn)

    def late(at, side):
        @pl.when(at < y)
        def _():
            late_now(at, side)

        @pl.when(at > y)
        def _():
            tmp[side] = jnp.zeros((2, GRAD, HEAD), F32)

    def red_copy(direction, step, sub, part):
        rows = pl.ds(part * RT, RT)
        return pltpu.make_async_remote_copy(
            src_ref=sb.at[direction, step, sub, rows], dst_ref=rb.at[direction, step, sub, rows],
            send_sem=red_s.at[direction, step, sub, part], recv_sem=red.at[direction, step, sub, part],
            device_id=ring_to[direction], device_id_type=MESH,
        )

    def red_here(direction, step, sub, part):
        rows = pl.ds(part * RT, RT)
        arrive(rb.at[direction, step, sub, rows], red.at[direction, step, sub, part])
        return rb[direction, step, sub, rows].astype(F32)

    def red_send(direction, step, sub, add, side):
        for part in (0, 1):
            rows = pl.ds(part * RT, RT)
            value = tmp[side, sub, rows]
            if add:
                value = value + red_here(direction, step - 1, sub, part)
            sb[direction, step, sub, rows] = value.astype(BF16)
            red_copy(direction, step, sub, part).start()

    red_order = ((0, 1), (1, 0), (0, 0), (1, 1))
    late(lax.rem(y + 4, 8), 0)
    for sub in (0, 1):
        red_send(sub, 0, sub, False, 0)
    for step in (1, 2, 3):

        @pl.loop(0, 2)
        def _(side):
            late(lax.rem(y + (4 - step) + side * 2 * (4 + step), 8), side)

        for direction, sub in red_order:
            red_send(direction, step, sub, step > 1 or direction == sub, direction)

    late_now(y, 0)

    dqx_out[:, 0:256] = dqt2[1 - c].astype(BF16)
    dqx_out[:, 256:384] = dqt3[1 - c].astype(BF16)
    send(dqx_out, dqx_in, xsem.at[1], sibling)
    arrive(dqx_in, xsem.at[1])
    query_two = (dqt2[c] + dqx_in[:, 0:256].astype(F32)) * SCALE
    query_three = (dqt3[c] + dqx_in[:, 256:384].astype(F32)) * SCALE
    rows_two, rows_three = query_two.T.astype(BF16), query_three.T.astype(BF16)

    def to_source(src, dst, sem, sub):
        to = device(y, 2 * c + sub, zh, x, zhalf)
        here = (z == 2 * c + sub) & (zhalf == c)
        keep(src, dst, sem, here)
        send(src, dst, sem, to, jnp.logical_not(here))

    for sub in (0, 1):
        dq_out[sub, 0:R2] = rows_two[sub * R2:(sub + 1) * R2]
        dq_out[sub, R2:RT] = rows_three[sub * R3:(sub + 1) * R3]
        to_source(dq_out.at[sub], dq_in.at[zpar], dqsem.at[zpar], sub)

    for part in (0, 1):
        rows = pl.ds(part * RT, RT)
        for sub in (0, 1):
            value = tmp[0, sub, rows]
            for direction in (sub, 1 - sub):
                value = value + red_here(direction, 3, sub, part)
            back_out[sub, rows] = value.astype(BF16)
            to_source(back_out.at[sub, rows], back_in.at[zpar, rows], backsem.at[zpar, part], sub)

    def results():
        for hh in (0, 1):
            yield dq_in.at[hh], dqsem.at[hh], dq_got.at[hh], outsem.at[hh]
        for part in (0, 1):
            rows = pl.ds(part * RT, RT)
            for hh in (0, 1):
                yield back_in.at[hh, rows], backsem.at[hh, part], back_got.at[hh, rows], outsem.at[2 + 2 * part + hh]

    for src, sem, dst, out_sem in results():
        arrive(src, sem)
        pltpu.make_async_copy(src, dst, out_sem).start()

    for copy, when in sent:
        if when is None:
            copy.wait_send()
        else:
            pl.when(when)(copy.wait_send)
    for copy in ring_sent:
        copy.wait_send()
    for step in range(4):
        for sub in (0, 1):
            for direction in (0, 1):
                if step > 0 or sub == direction:
                    for part in (0, 1):
                        red_copy(direction, step, sub, part).wait_send()
    for src, _, dst, out_sem in results():
        pltpu.make_async_copy(src, dst, out_sem).wait()


def lay_out(dq_got, back_got, dq2, dk2, dv2, dq3, dk3, dv3, sem):
    copies = []
    for hh in (0, 1):
        cols = pl.ds(hh * HEAD, HEAD)
        parts = (
            (back_got.at[hh, 0:R2], dk2),
            (back_got.at[hh, RT:RT + R2], dv2),
            (dq_got.at[hh, 0:R2], dq2),
            (back_got.at[hh, R2:RT], dk3),
            (back_got.at[hh, RT + R2:GRAD], dv3),
            (dq_got.at[hh, R2:RT], dq3),
        )
        for src, dst in parts:
            copies.append(pltpu.make_async_copy(src, dst.at[:, cols], sem.at[len(copies)]))
    for copy in copies:
        copy.start()
    for copy in copies:
        copy.wait()


def on_device(q2, k2, v2, cot2, kept2, q3, k3, v3, cot3, kept3, weight):
    hbm = pl.BlockSpec(memory_space=pltpu.HBM)
    dma = pltpu.SemaphoreType.DMA
    line2 = kept2.reshape(1, R2)
    line3 = kept3.reshape(1, R3)
    got = pl.pallas_call(
        body,
        out_shape=(
            jax.ShapeDtypeStruct((2, RT, HEAD), BF16),
            jax.ShapeDtypeStruct((2, GRAD, HEAD), BF16),
        ),
        in_specs=[hbm] * 11,
        out_specs=(hbm,) * 2,
        scratch_shapes=[
            pltpu.VMEM((2, 4, 2 * FEAT, R2), BF16),
            pltpu.VMEM((2, 4, 2, R3, FEAT), BF16),
            pltpu.VMEM((1, R2), jnp.int32),
            pltpu.VMEM((1, R3), jnp.int32),
            pltpu.VMEM((2 * HEAD, 16 * FEAT), BF16),
            pltpu.VMEM((8, 2, SLOT, HEAD), BF16),
            pltpu.VMEM((512, HEAD), BF16),
            pltpu.VMEM((256, HEAD), BF16),
            pltpu.VMEM((HEAD, 512), BF16),
            pltpu.VMEM((HEAD, 256), BF16),
            pltpu.VMEM((HEAD, 512), BF16),
            pltpu.VMEM((256, HEAD), BF16),
            pltpu.VMEM((16, HEAD), BF16),
            pltpu.VMEM((2 * HEAD, R2), F32),
            pltpu.VMEM((2 * HEAD, R3), F32),
            pltpu.VMEM((2, HEAD, R2), BF16),
            pltpu.VMEM((2, R3, HEAD), BF16),
            pltpu.VMEM((HEAD, 512), F32),
            pltpu.VMEM((HEAD, 256), F32),
            pltpu.VMEM((8, 2 * R2, 512), F32),
            pltpu.VMEM((8, 2 * R3, 256), F32),
            pltpu.VMEM((8, 768), F32),
            pltpu.VMEM((8, 768), F32),
            pltpu.VMEM((8, 768), F32),
            pltpu.VMEM((2, 4, 2, GRAD, HEAD), BF16),
            pltpu.VMEM((2, 4, 2, GRAD, HEAD), BF16),
            pltpu.VMEM((2, 2, GRAD, HEAD), F32),
            pltpu.VMEM((2, HEAD, 256), F32),
            pltpu.VMEM((2, HEAD, 128), F32),
            pltpu.VMEM((HEAD, 384), BF16),
            pltpu.VMEM((HEAD, 384), BF16),
            pltpu.VMEM((2, RT, HEAD), BF16),
            pltpu.VMEM((2, RT, HEAD), BF16),
            pltpu.VMEM((2, GRAD, HEAD), BF16),
            pltpu.VMEM((2, GRAD, HEAD), BF16),
            dma((80,)),
            dma((5,)),
            dma((2,)),
            dma((2, 2, 4)),
            dma((2, 2, 4)),
            dma((2,)),
            dma((4, 2)),
            dma((4, 2)),
            dma((2, 4, 2)),
            dma((2, 4, 2, 2)),
            dma((2, 4, 2)),
            dma((2, 4, 2, 2)),
            dma((2,)),
            dma((2, 2)),
            dma((2,)),
            dma((6,)),
        ],
        compiler_params=pltpu.CompilerParams(
            collective_id=0, has_side_effects=True, vmem_limit_bytes=64 * 1024 * 1024
        ),
        name="attention_backward",
    )(line2, line3, q2, k2, v2, cot2.T, q3, k3, v3, cot3, weight)
    wide = jax.ShapeDtypeStruct((R2, 2 * HEAD), BF16)
    narrow = jax.ShapeDtypeStruct((R3, 2 * HEAD), BF16)
    return pl.pallas_call(
        lay_out,
        out_shape=(wide, wide, wide, narrow, narrow, narrow),
        in_specs=[pl.BlockSpec(memory_space=pltpu.VMEM)] * 2,
        out_specs=(hbm,) * 6,
        scratch_shapes=[dma((12,))],
        name="lay_out",
    )(*got)


def solution(mesh):
    shard = P("seq", "tp")
    in_specs = (shard, shard, shard, shard, P("seq"), shard, shard, shard, shard, P("seq"), P("tp", None))
    return jax.shard_map(on_device, mesh=mesh, in_specs=in_specs, out_specs=(shard,) * 6, check_vma=False)
```
